32 devices in a mesh: row: 16 (over z, x, core), col: 2 (over y).
Axes of the slice: x: 2, y: 2, z: 4, core: 2. Of those that a mesh axis runs over, the one named last changes fastest.
Arguments:
- tokens: bfloat16 [6144, 2560], P('row', 'col'), may hold values from -8 to 8
- dest_row: int32 [6144], P('row'), may hold values from 0 to 14335, as said below
- seq_lens: int32 [16, 4], P('row'), may hold values from 0 to 384, as said below
- cotangent: bfloat16 [14336, 2560], P('row', 'col'), may hold values from -8 to 8
- query_down: float32 [2560, 768], P('row'), may hold values from -0.125 to 0.125
- joint_down: float32 [2560, 288], P('row'), may hold values from -0.125 to 0.125
- query_up: float32 [768, 3840], P('row', 'col'), may hold values from -0.3125 to 0.3125
- joint_up: float32 [256, 5120], P('row', 'col'), may hold values from -0.375 to 0.375
- out_weight: float32 [2560, 2560], P('row', 'col'), may hold values from -2.5 to 2.5
- gate_weight: float32 [2560, 6400], P('row', 'col'), may hold values from -0.125 to 0.125
- up_weight: float32 [2560, 6400], P('row', 'col'), may hold values from -0.125 to 0.125
- down_weight: float32 [2560, 6400], P('row', 'col'), may hold values from -0.625 to 0.625
- norm_gains: float32 [6144], P('row'), may hold values from 0.5 to 1.5
- first_query_down: float32 [2560, 768], P('row'), may hold values from -112 to 112
- first_joint_down: float32 [2560, 288], P('row'), may hold values from -160 to 160
- first_query_up: float32 [768, 3840], P('row', 'col'), may hold values from -56 to 56
- first_joint_up: float32 [256, 5120], P('row', 'col'), may hold values from -56 to 56
- first_out_weight: float32 [2560, 2560], P('row', 'col'), may hold values from -4 to 4
- first_gate_weight: float32 [2560, 6400], P('row', 'col'), may hold values from -28 to 28
- first_up_weight: float32 [2560, 6400], P('row', 'col'), may hold values from -28 to 28
- first_down_weight: float32 [2560, 6400], P('row', 'col'), may hold values from -4 to 4
- first_norm_gains: float32 [6144], P('row'), may hold values from -80 to 80
- second_query_down: float32 [2560, 768], P('row'), may hold values from 1290.24 to 5160.96
- second_joint_down: float32 [2560, 288], P('row'), may hold values from 2887.68 to 11673.6
- second_query_up: float32 [768, 3840], P('row', 'col'), may hold values from 325.632 to 1290.24
- second_joint_up: float32 [256, 5120], P('row', 'col'), may hold values from 325.632 to 1290.24
- second_out_weight: float32 [2560, 2560], P('row', 'col'), may hold values from 0.811008 to 3.2256
- second_gate_weight: float32 [2560, 6400], P('row', 'col'), may hold values from 103.41581 to 412.8768
- second_up_weight: float32 [2560, 6400], P('row', 'col'), may hold values from 103.41581 to 412.8768
- second_down_weight: float32 [2560, 6400], P('row', 'col'), may hold values from 3.231744 to 12.9024
- second_norm_gains: float32 [6144], P('row'), may hold values from 724.992 to 2887.68
Outputs:
- outputs: bfloat16 [14336, 2560], P('row', 'col')
- grad_tokens: bfloat16 [6144, 2560], P('row', 'col')
- grad_query_down: float32 [2560, 768], P('row')
- grad_joint_down: float32 [2560, 288], P('row')
- grad_query_up: float32 [768, 3840], P('row', 'col')
- grad_joint_up: float32 [256, 5120], P('row', 'col')
- grad_out_weight: float32 [2560, 2560], P('row', 'col')
- grad_gate_weight: float32 [2560, 6400], P('row', 'col')
- grad_up_weight: float32 [2560, 6400], P('row', 'col')
- grad_down_weight: float32 [2560, 6400], P('row', 'col')
- grad_norm_gains: float32 [6144], P('row')
- second_query_down_next: float32 [2560, 768], P('row')
- second_joint_down_next: float32 [2560, 288], P('row')
- second_query_up_next: float32 [768, 3840], P('row', 'col')
- second_joint_up_next: float32 [256, 5120], P('row', 'col')
- second_out_weight_next: float32 [2560, 2560], P('row', 'col')
- second_gate_weight_next: float32 [2560, 6400], P('row', 'col')
- second_up_weight_next: float32 [2560, 6400], P('row', 'col')
- second_down_weight_next: float32 [2560, 6400], P('row', 'col')
- second_norm_gains_next: float32 [6144], P('row')
- query_down_next: float32 [2560, 768], P('row')
- joint_down_next: float32 [2560, 288], P('row')
- query_up_next: float32 [768, 3840], P('row', 'col')
- joint_up_next: float32 [256, 5120], P('row', 'col')
- out_weight_next: float32 [2560, 2560], P('row', 'col')
- gate_weight_next: float32 [2560, 6400], P('row', 'col')
- up_weight_next: float32 [2560, 6400], P('row', 'col')
- down_weight_next: float32 [2560, 6400], P('row', 'col')
- norm_gains_next: float32 [6144], P('row')
The draws below stay inside these ranges and needn't reach their ends.
Inputs may be any that keep to these rules, and one draw needn't show every extreme that they name: `seq_lens`: row g lists the lengths of the sequences of group g in layout order and sums to 384; one row, drawn from the seed, is 384 followed by zeros. `dest_row`: group g owns rows g * 896 to (g + 1) * 896 - 1 of the balanced layout; its sequences stand there in the order of seq_lens row g, each preceded by the fewest empty rows that make its extent a multiple of 128, the last ending at the group's last row, the remaining empty rows before the first. Each token has a distinct row, every occupied row belongs to a token, and the 384 tokens of each device along row hold exactly 24 tokens of every group.
All inputs are finite; a program needn't handle non-finite values.
Results may differ from the reference program's by a relative error of at most 0.03.
Values may be sent and summed in bfloat16 or wider, within the bound.
No kernel may reach another device: no remote copies, remote signals or barrier semaphores. Data moves between devices by JAX's collectives and lax.ppermute only.
A program may use at most 320 MiB of HBM per device.

```python
import math
import jax
import jax.numpy as jnp
from jax import lax

D = 2560
FF = 6400
HEADS = 40
NOPE = 64
ROPE = 32
VDIM = 64
Q_RANK = 768
KV_RANK = 256
TOK_DEV = 384
SEQS = 4
BLK = 128
STEP = 10
GROUPS = 16
SHARE = 24
CAP = 896
TOKENS = 6144
PADDED = 14336
GAINS = 6144


def layout_drawn(lengths):
    lengths = lengths.astype(jnp.int32)
    padded = ((lengths + BLK - 1) // BLK * BLK).astype(jnp.int32)
    endings = (CAP - jnp.sum(padded) + jnp.cumsum(padded)).astype(jnp.int32)
    starts = (endings - lengths).astype(jnp.int32)
    row_ids = jnp.arange(CAP, dtype=jnp.int32)
    inside = (row_ids[:, None] >= starts[None, :]) & (row_ids[:, None] < endings[None, :])
    labels = jnp.arange(SEQS, dtype=jnp.int32) + 1
    segment = (jnp.sum(jnp.where(inside, labels[None, :], 0), axis=1) - 1).astype(jnp.int32)
    return segment


def balanced_layout(key):
    key_lengths, key_single, key_groups, key_sources = jax.random.split(key, 4)
    cut_points = jnp.sort(jax.random.randint(key_lengths, (GROUPS, SEQS - 1), 0, TOK_DEV + 1), axis=1).astype(jnp.int32)
    boundary = jnp.concatenate([jnp.zeros((GROUPS, 1), jnp.int32), cut_points, jnp.full((GROUPS, 1), TOK_DEV, jnp.int32)], axis=1)
    lengths = boundary[:, 1:] - boundary[:, :-1]
    chosen = jax.random.randint(key_single, (), 0, GROUPS)
    lone_group = jnp.zeros((SEQS,), jnp.int32).at[0].set(TOK_DEV)
    lengths = jnp.where((jnp.arange(GROUPS) == chosen)[:, None], lone_group[None, :], lengths).astype(jnp.int32)
    segment = jax.vmap(layout_drawn)(lengths)
    empty_flag = (segment < 0).astype(jnp.int32)
    occupied = jnp.argsort(empty_flag, axis=1, stable=True)[:, :TOK_DEV].astype(jnp.int32)
    group_keys = jax.random.split(key_groups, GROUPS)
    shuffled = jax.vmap(lambda one_key, group_rows: group_rows[jax.random.permutation(one_key, TOK_DEV)])(group_keys, occupied)
    shuffled = shuffled + (jnp.arange(GROUPS, dtype=jnp.int32) * CAP)[:, None]
    per_source = jnp.transpose(shuffled.reshape(GROUPS, GROUPS, SHARE), (1, 0, 2)).reshape(GROUPS, TOK_DEV)
    source_keys = jax.random.split(key_sources, GROUPS)
    mixed = jax.vmap(lambda one_key, source_rows: source_rows[jax.random.permutation(one_key, TOK_DEV)])(source_keys, per_source)
    return (lengths, mixed.reshape(TOKENS).astype(jnp.int32))


def draw_seq_lens(key, part):
    return balanced_layout(key)[0]


def draw_dest_row(key, part):
    return balanced_layout(key)[1]


def draw_tokens(key, part):
    key = jax.random.fold_in(key, 11)
    column = jnp.arange(D, dtype=jnp.float32) / max(D - 1, 1)
    base = jnp.clip(jax.random.normal(key, (TOKENS, D), jnp.float32), -4.0, 4.0)
    column_scale = 0.6 + 1.2 * column
    return (base * column_scale[None, :]).astype(jnp.bfloat16)


def draw_cotangent(key, part):
    key = jax.random.fold_in(key, 23)
    row_place = jnp.arange(PADDED, dtype=jnp.float32) / max(PADDED - 1, 1)
    base = jnp.clip(jax.random.normal(key, (PADDED, D), jnp.float32), -4.0, 4.0)
    row_scale = 0.6 + 1.2 * row_place
    return (base * row_scale[:, None]).astype(jnp.bfloat16)


def block_scale(key, dims, shards, smallest, high):
    factor_of = 1.0
    for dim, shards_of in shards:
        heights = jax.random.uniform(jax.random.fold_in(jax.random.fold_in(key, 6), dim), (shards_of,), jnp.float32, smallest / len(shards), high / len(shards))
        factor_of = factor_of * jnp.repeat(jnp.exp(heights), dims[dim] // shards_of).reshape((-1,) + (1,) * (len(dims) - 1 - dim))
    return factor_of


def centred(stream_key, extent, spread, reach, cuts=(), kind=jnp.bfloat16):
    values = jax.random.normal(stream_key, extent, jnp.float32) * spread
    if len(cuts) > 0:
        values = block_scale(stream_key, extent, cuts, -0.22, 0.18) * values
    return jnp.clip(values, min=-reach, max=reach).astype(kind)


def setup_inputs(seed: int = 0) -> dict:
    splits = jax.random.split(jax.random.key(seed), 32)
    return {
        "tokens": draw_tokens(jax.random.fold_in(splits[31], 71), 0),
        "dest_row": draw_dest_row(jax.random.fold_in(splits[31], 71), 0),
        "seq_lens": draw_seq_lens(jax.random.fold_in(splits[31], 71), 0),
        "cotangent": draw_cotangent(jax.random.fold_in(splits[31], 71), 0),
        "query_down": centred(splits[4], (D, Q_RANK), D ** -0.5, 0.125, ((0, 16),), jnp.float32),
        "joint_down": centred(splits[5], (D, KV_RANK + ROPE), D ** -0.5, 0.125, ((0, 16),), jnp.float32),
        "query_up": centred(splits[6], (Q_RANK, HEADS * (NOPE + ROPE)), (Q_RANK // 2) ** -0.5, 0.3125, ((0, 16), (1, 2)), jnp.float32),
        "joint_up": centred(splits[7], (KV_RANK, HEADS * (NOPE + VDIM)), KV_RANK ** -0.5, 0.375, ((0, 16), (1, 2)), jnp.float32),
        "out_weight": centred(splits[8], (D, HEADS * VDIM), (max(HEADS * VDIM // 512, 1)) ** -0.5, 2.5, ((0, 16), (1, 2)), jnp.float32),
        "gate_weight": centred(splits[9], (D, FF), D ** -0.5, 0.125, ((0, 16), (1, 2)), jnp.float32),
        "up_weight": centred(splits[10], (D, FF), D ** -0.5, 0.125, ((0, 16), (1, 2)), jnp.float32),
        "down_weight": centred(splits[11], (D, FF), (max(FF // 80, 1)) ** -0.5, 0.625, ((0, 16), (1, 2)), jnp.float32),
        "norm_gains": jnp.clip(1.0 + 0.1 * jax.random.normal(splits[12], (GAINS,), jnp.float32), 0.5, 1.5),
        "first_query_down": centred(splits[13], (D, Q_RANK), (0.22 * TOKENS ** 0.5), 112.0, ((0, 16),), jnp.float32),
        "first_joint_down": centred(splits[14], (D, KV_RANK + ROPE), (0.33 * TOKENS ** 0.5), 160.0, ((0, 16),), jnp.float32),
        "first_query_up": centred(splits[15], (Q_RANK, HEADS * (NOPE + ROPE)), (0.11 * TOKENS ** 0.5), 56.0, ((0, 16), (1, 2)), jnp.float32),
        "first_joint_up": centred(splits[16], (KV_RANK, HEADS * (NOPE + VDIM)), (0.11 * TOKENS ** 0.5), 56.0, ((0, 16), (1, 2)), jnp.float32),
        "first_out_weight": centred(splits[17], (D, HEADS * VDIM), (0.0056 * TOKENS ** 0.5), 4.0, ((0, 16), (1, 2)), jnp.float32),
        "first_gate_weight": centred(splits[18], (D, FF), (0.011 * (D * TOKENS / max(FF // 80, 1)) ** 0.5), 28.0, ((0, 16), (1, 2)), jnp.float32),
        "first_up_weight": centred(splits[19], (D, FF), (0.011 * (D * TOKENS / max(FF // 80, 1)) ** 0.5), 28.0, ((0, 16), (1, 2)), jnp.float32),
        "first_down_weight": centred(splits[20], (D, FF), (0.011 * TOKENS ** 0.5), 4.0, ((0, 16), (1, 2)), jnp.float32),
        "first_norm_gains": centred(splits[21], (GAINS,), (0.167 * TOKENS ** 0.5), 80.0, ((0, 16),), jnp.float32),
        "second_query_down": jnp.clip(jnp.exp(math.log(5160.96) - 1.3862944 * jax.random.uniform(splits[22], (D, Q_RANK), jnp.float32) ** block_scale(splits[22], (D, Q_RANK), ((0, 16),), -0.2, 0.2)), 1290.24, 5160.96),
        "second_joint_down": jnp.clip(jnp.exp(math.log(11673.6) - 1.3968765 * jax.random.uniform(splits[23], (D, KV_RANK + ROPE), jnp.float32) ** block_scale(splits[23], (D, KV_RANK + ROPE), ((0, 16),), -0.2, 0.2)), 2887.68, 11673.6),
        "second_query_up": jnp.clip(jnp.exp(math.log(1290.24) - 1.37681564 * jax.random.uniform(splits[24], (Q_RANK, HEADS * (NOPE + ROPE)), jnp.float32) ** block_scale(splits[24], (Q_RANK, HEADS * (NOPE + ROPE)), ((0, 16), (1, 2)), -0.2, 0.2)), 325.632, 1290.24),
        "second_joint_up": jnp.clip(jnp.exp(math.log(1290.24) - 1.37681564 * jax.random.uniform(splits[25], (KV_RANK, HEADS * (NOPE + VDIM)), jnp.float32) ** block_scale(splits[25], (KV_RANK, HEADS * (NOPE + VDIM)), ((0, 16), (1, 2)), -0.2, 0.2)), 325.632, 1290.24),
        "second_out_weight": jnp.clip(jnp.exp(math.log(3.2256) - 1.3805964 * jax.random.uniform(splits[26], (D, HEADS * VDIM), jnp.float32) ** block_scale(splits[26], (D, HEADS * VDIM), ((0, 16), (1, 2)), -0.2, 0.2)), 0.811008, 3.2256),
        "second_gate_weight": jnp.clip(jnp.exp(math.log(412.8768) - 1.3843914 * jax.random.uniform(splits[27], (D, FF), jnp.float32) ** block_scale(splits[27], (D, FF), ((0, 16), (1, 2)), -0.2, 0.2)), 103.41581, 412.8768),
        "second_up_weight": jnp.clip(jnp.exp(math.log(412.8768) - 1.3843914 * jax.random.uniform(splits[28], (D, FF), jnp.float32) ** block_scale(splits[28], (D, FF), ((0, 16), (1, 2)), -0.2, 0.2)), 103.41581, 412.8768),
        "second_down_weight": jnp.clip(jnp.exp(math.log(12.9024) - 1.3843914 * jax.random.uniform(splits[29], (D, FF), jnp.float32) ** block_scale(splits[29], (D, FF), ((0, 16), (1, 2)), -0.2, 0.2)), 3.231744, 12.9024),
        "second_norm_gains": jnp.clip(jnp.exp(math.log(2887.68) - 1.382048 * jax.random.uniform(splits[30], (GAINS,), jnp.float32) ** block_scale(splits[30], (GAINS,), ((0, 16),), -0.2, 0.2)), 724.992, 2887.68),
    }


EPSILON = 1e-05
RESIDUAL_SCALE = 1.4 / 62 ** 0.5
BETA_ONE = 0.9
BETA_TWO = 0.95
ADAM_EPSILON = 1e-08
DECAY_RATE = 0.1
MASKED = -1e+30
HIGHEST = lax.Precision.HIGHEST

@jax.custom_vjp
def low(v):
    return lax.optimization_barrier(v.astype(jnp.bfloat16)).astype(jnp.float32)

@jax.custom_vjp
def low_back(v):
    return v

def low_keep(v):
    return (low(v), None)

def low_pass(kept, grad):
    return (grad,)

def back_keep(v):
    return (v, None)

def back_low(kept, grad):
    return (low(grad),)
low.defvjp(low_keep, low_pass)
low_back.defvjp(back_keep, back_low)

def layout(lengths):
    lengths = lengths.astype(jnp.int32)
    padded = ((lengths + BLK - 1) // BLK * BLK).astype(jnp.int32)
    endings = (CAP - jnp.sum(padded) + jnp.cumsum(padded)).astype(jnp.int32)
    starts = (endings - lengths).astype(jnp.int32)
    row_ids = jnp.arange(CAP, dtype=jnp.int32)
    inside = (row_ids[:, None] >= starts[None, :]) & (row_ids[:, None] < endings[None, :])
    labels = jnp.arange(SEQS, dtype=jnp.int32) + 1
    segment = (lax.optimization_barrier(jnp.sum(jnp.where(inside, labels[None, :], 0), axis=1)) - 1).astype(jnp.int32)
    position = lax.optimization_barrier(jnp.sum(jnp.where(inside, row_ids[:, None] - starts[None, :], 0), axis=1)).astype(jnp.int32)
    return (segment, position)

def rotary_tables(position):
    frequency = 10000.0 ** (-(jnp.arange(ROPE // 2, dtype=jnp.float32) * 2.0 / ROPE))
    angles = position.astype(jnp.float32)[:, None] * frequency[None, :]
    cosine = jnp.concatenate([jnp.cos(angles), jnp.cos(angles)], axis=1)
    sine_table = jnp.concatenate([jnp.sin(angles), jnp.sin(angles)], axis=1)
    return (cosine, sine_table)

def rotate_half(values):
    half_width = values.shape[-1] // 2
    return jnp.concatenate([-values[..., half_width:], values[..., :half_width]], axis=-1)

def apply_rotary(values, cosine, sine_table):
    return values * cosine + rotate_half(values) * sine_table

def rms_norm(values, gain_values):
    return values * lax.rsqrt(lax.optimization_barrier(jnp.mean(values * values, axis=-1, keepdims=True)) + EPSILON) * gain_values

def matmul(left_side, right_side):
    return jnp.dot(left_side, right_side, precision=HIGHEST)

def head_attention(head_pair, key_rope, segment):
    queries, joint_rows = head_pair
    row_ids = jnp.arange(CAP, dtype=jnp.int32)
    raw_scores = (matmul(queries[:, :NOPE], joint_rows[:, :NOPE].T) + matmul(queries[:, NOPE:], key_rope.T)) * (NOPE + ROPE) ** (-0.5)
    valid_pairs = (segment[:, None] == segment[None, :]) & (segment[:, None] >= 0) & (row_ids[None, :] <= row_ids[:, None])
    scores = low_back(jnp.where(valid_pairs, raw_scores, MASKED))
    prob_rows = low(jax.nn.softmax(scores, axis=-1))
    return matmul(prob_rows, joint_rows[:, NOPE:])

def group_forward(inputs, params, segment, cosine, sine_table):
    query_down, joint_down, query_up, joint_up, out_weight, gate_weight, up_weight, down_weight, norm_gains = [low(param_value) for param_value in params]
    gain_one = norm_gains[:D]
    gain_two = norm_gains[D:2 * D]
    gain_query = norm_gains[2 * D:2 * D + Q_RANK]
    gain_joint = norm_gains[2 * D + Q_RANK:]
    normed_one = low(rms_norm(inputs, gain_one))
    query_latent = low_back(matmul(normed_one, query_down))
    joint_latent = low_back(matmul(normed_one, joint_down))
    query_normed = low(rms_norm(query_latent, gain_query))
    compressed = low(rms_norm(joint_latent[:, :KV_RANK], gain_joint))
    key_rope = low(apply_rotary(joint_latent[:, KV_RANK:], cosine, sine_table))
    query_full = low_back(matmul(query_normed, query_up)).reshape(CAP, HEADS, NOPE + ROPE)
    queries = low(jnp.concatenate([query_full[..., :NOPE], apply_rotary(query_full[..., NOPE:], cosine[:, None, :], sine_table[:, None, :])], axis=-1))
    joint_full = low(low_back(matmul(compressed, joint_up))).reshape(CAP, HEADS, NOPE + VDIM)
    per_head = lax.map(jax.checkpoint(lambda head_pair: head_attention(head_pair, key_rope, segment)), (jnp.transpose(queries, (1, 0, 2)), jnp.transpose(joint_full, (1, 0, 2))))
    attended = low(low_back(jnp.transpose(per_head, (1, 0, 2)).reshape(CAP, HEADS * VDIM)))
    branch = low_back(matmul(attended, out_weight.T))
    residual = inputs + RESIDUAL_SCALE * branch
    normed_two = low(rms_norm(residual, gain_two))
    gate_rows = low_back(matmul(normed_two, gate_weight))
    up_rows = low_back(matmul(normed_two, up_weight))
    activated = low(jax.nn.silu(gate_rows) * up_rows)
    feed_forward = low_back(matmul(activated, down_weight.T))
    return residual + RESIDUAL_SCALE * feed_forward

def learning_rates():
    return (3.0 * D ** (-0.5), 3.0 * D ** (-0.5), 3.0 * (Q_RANK // 2) ** (-0.5), 3.0 * KV_RANK ** (-0.5), 3.0 * max(HEADS * VDIM // 512, 1) ** (-0.5), 3.0 * D ** (-0.5), 3.0 * D ** (-0.5), 3.0 * max(FF // 80, 1) ** (-0.5), 0.6)

def adam_update(weight_old, grad_value, first_old, second_old, step_rate):
    first_new = BETA_ONE * first_old + (1.0 - BETA_ONE) * grad_value
    second_new = BETA_TWO * second_old + (1.0 - BETA_TWO) * grad_value * grad_value
    first_hat = first_new / (1.0 - BETA_ONE ** STEP)
    second_hat = second_new / (1.0 - BETA_TWO ** STEP)
    weight_new = weight_old - step_rate * (first_hat / (jnp.sqrt(second_hat) + ADAM_EPSILON) + DECAY_RATE * weight_old)
    return (second_new, weight_new)

def reference(tokens, dest_row, seq_lens, cotangent, query_down, joint_down, query_up, joint_up, out_weight, gate_weight, up_weight, down_weight, norm_gains, first_query_down, first_joint_down, first_query_up, first_joint_up, first_out_weight, first_gate_weight, first_up_weight, first_down_weight, first_norm_gains, second_query_down, second_joint_down, second_query_up, second_joint_up, second_out_weight, second_gate_weight, second_up_weight, second_down_weight, second_norm_gains):
    params = (query_down, joint_down, query_up, joint_up, out_weight, gate_weight, up_weight, down_weight, norm_gains)
    firsts = (first_query_down, first_joint_down, first_query_up, first_joint_up, first_out_weight, first_gate_weight, first_up_weight, first_down_weight, first_norm_gains)
    seconds = (second_query_down, second_joint_down, second_query_up, second_joint_up, second_out_weight, second_gate_weight, second_up_weight, second_down_weight, second_norm_gains)
    placed = jnp.zeros((PADDED, D), jnp.float32).at[dest_row].set(tokens.astype(jnp.float32))

    def group_step(totals, group_inputs):
        group_tokens, group_upstream, lengths = group_inputs
        segment, position = layout(lengths)
        cosine, sine_table = rotary_tables(position)
        occupied = (segment >= 0).astype(jnp.float32)[:, None]

        def forward_fn(inputs, weights):
            return group_forward(inputs, weights, segment, cosine, sine_table)
        block_out, pullback = jax.vjp(forward_fn, group_tokens, params)
        grad_inputs, grad_params = pullback(group_upstream * occupied)
        totals = jax.tree.map(lambda left_side, right_side: left_side + right_side, totals, grad_params)
        return (totals, (block_out * occupied, grad_inputs))
    zero_grads = tuple((jnp.zeros_like(param_value) for param_value in params))
    totals, (block_out, grad_inputs) = lax.scan(group_step, zero_grads, (placed.reshape(GROUPS, CAP, D), cotangent.astype(jnp.float32).reshape(GROUPS, CAP, D), seq_lens))
    result_rows = block_out.reshape(PADDED, D).astype(jnp.bfloat16)
    grad_tokens = grad_inputs.reshape(PADDED, D)[dest_row].astype(jnp.bfloat16)
    step_rates = learning_rates()
    seconds_next = []
    weights_next = []
    for slot_index in range(9):
        second_new, weight_new = adam_update(params[slot_index], totals[slot_index], firsts[slot_index], seconds[slot_index], step_rates[slot_index])
        seconds_next.append(second_new)
        weights_next.append(weight_new)
    return (result_rows, grad_tokens, totals[0], totals[1], totals[2], totals[3], totals[4], totals[5], totals[6], totals[7], totals[8], seconds_next[0], seconds_next[1], seconds_next[2], seconds_next[3], seconds_next[4], seconds_next[5], seconds_next[6], seconds_next[7], seconds_next[8], weights_next[0], weights_next[1], weights_next[2], weights_next[3], weights_next[4], weights_next[5], weights_next[6], weights_next[7], weights_next[8])
```

```python
import functools

import jax
import jax.numpy as jnp
from jax import lax
from jax.experimental import pallas as pl
from jax.experimental.pallas import tpu as pltpu
from jax.sharding import PartitionSpec as P

D = 2560
FF = 6400
HEADS = 40
NOPE = 64
ROPE = 32
VDIM = 64
Q_RANK = 768
KV_RANK = 256
SEQS = 4
BLK = 128
STEP = 10
CAP = 896

Z_SIZE = 4
CORES = 2

EPSILON = 1e-05
RESIDUAL_SCALE = 1.4 / 62**0.5
BETA_ONE = 0.9
BETA_TWO = 0.95
ADAM_EPSILON = 1e-08
DECAY_RATE = 0.1
MASKED = -1e30
SCORE_SCALE = (NOPE + ROPE) ** (-0.5)
FULL_TYPE = jnp.float32
HALF_TYPE = jnp.bfloat16


def rms_scale(values):
    return lax.rsqrt(jnp.mean(values * values, axis=-1, keepdims=True) + EPSILON)


def rms_backward(grad_normed, values, norm_scale, gain_values):
    weighted = grad_normed * gain_values
    mean_term = jnp.mean(weighted * values, axis=-1, keepdims=True)
    grad_values = norm_scale * weighted - values * norm_scale**3 * mean_term
    grad_gain = jnp.sum(grad_normed * values * norm_scale, axis=0)
    return (grad_values, grad_gain)


def product(left_side, right_side):
    return jnp.dot(left_side, right_side, preferred_element_type=FULL_TYPE)


def contract_rows(left_side, right_side):
    return lax.dot_general(
        left_side, right_side, (((0,), (0,)), ((), ())), preferred_element_type=FULL_TYPE
    )


def times_transposed(left_side, right_side):
    return lax.dot_general(
        left_side, right_side, (((1,), (1,)), ((), ())), preferred_element_type=FULL_TYPE
    )


def rotate_half(values):
    half_width = values.shape[-1] // 2
    return jnp.concatenate([-values[..., half_width:], values[..., :half_width]], axis=-1)


def rotate_back(values):
    half_width = values.shape[-1] // 2
    return jnp.concatenate([values[..., half_width:], -values[..., :half_width]], axis=-1)


def learning_rates():
    return (
        3.0 * D ** (-0.5),
        3.0 * D ** (-0.5),
        3.0 * (Q_RANK // 2) ** (-0.5),
        3.0 * KV_RANK ** (-0.5),
        3.0 * max(HEADS * VDIM // 512, 1) ** (-0.5),
        3.0 * D ** (-0.5),
        3.0 * D ** (-0.5),
        3.0 * max(FF // 80, 1) ** (-0.5),
        0.6,
    )


def adam_update(weight_old, grad_value, first_old, second_old, step_rate):
    first_new = BETA_ONE * first_old + (1.0 - BETA_ONE) * grad_value
    second_new = BETA_TWO * second_old + (1.0 - BETA_TWO) * grad_value * grad_value
    first_hat = first_new / (1.0 - BETA_ONE**STEP)
    second_hat = second_new / (1.0 - BETA_TWO**STEP)
    weight_new = weight_old - step_rate * (
        first_hat / (jnp.sqrt(second_hat) + ADAM_EPSILON) + DECAY_RATE * weight_old
    )
    return (second_new, weight_new)


def turn_matrix(width):
    rows = lax.broadcasted_iota(jnp.int32, (width, width), 0)
    columns = lax.broadcasted_iota(jnp.int32, (width, width), 1)
    half = ROPE // 2
    in_first = (columns % ROPE) < half
    minus = in_first & (rows == columns + half)
    plus = jnp.logical_not(in_first) & (rows == columns - half)
    return jnp.where(plus, 1.0, jnp.where(minus, -1.0, 0.0)).astype(HALF_TYPE)


def split_dot(values, matrix, dims):
    high = values.astype(HALF_TYPE)
    low = (values - high.astype(FULL_TYPE)).astype(HALF_TYPE)
    dot = functools.partial(
        lax.dot_general, dimension_numbers=(dims, ((), ())), preferred_element_type=FULL_TYPE
    )
    return dot(high, matrix) + dot(low, matrix)


NT = ((1,), (1,))
NN = ((1,), (0,))


def kernel_dot(left_side, right_side, dims):
    return lax.dot_general(
        left_side, right_side, (dims, ((), ())), preferred_element_type=FULL_TYPE
    )


def fill_bias(bias_ref, row_here, row_across, first_across):
    key_rows = row_here[...]
    allowed = (key_rows >= first_across[...]) & (key_rows <= row_across[...])
    bias_ref[...] = jnp.where(allowed, 0.0, MASKED)


def attend_kernel(
    group,
    row_here,
    row_across,
    first_across,
    cosine,
    sine,
    key_rope,
    query_nope,
    query_rope,
    joint,
    attended,
    rotated,
    totals,
    bias,
):
    @pl.when(pl.program_id(0) == 0)
    def _():
        fill_bias(bias, row_here, row_across, first_across)

    turn = turn_matrix(group * ROPE)
    rope_in = query_rope[...]
    rotated[...] = (
        rope_in * cosine[...] + split_dot(rope_in, turn, NN) * sine[...]
    ).astype(HALF_TYPE)
    rope_keys = key_rope[...]
    for head in range(group):
        keys = joint[:, head * 128 : head * 128 + NOPE]
        values = joint[:, head * 128 + NOPE : (head + 1) * 128]
        scores = (
            kernel_dot(keys, query_nope[:, head * NOPE : (head + 1) * NOPE], NT)
            + kernel_dot(rope_keys, rotated[:, head * ROPE : (head + 1) * ROPE], NT)
        ) * SCORE_SCALE + bias[...]
        top = jnp.max(scores, axis=0, keepdims=True)
        powers = jnp.exp(scores - top)
        total = jnp.sum(powers, axis=0, keepdims=True)
        weights = (powers * (1.0 / total)).astype(HALF_TYPE)
        found = kernel_dot(values.T, weights, NN)
        attended[:, head * VDIM : (head + 1) * VDIM] = found.T.astype(HALF_TYPE)
        totals[0, head : head + 1, :] = top + jnp.log(total)


def attend_back_kernel(
    group,
    row_here,
    row_across,
    first_across,
    cosine,
    sine,
    key_rope,
    query_nope,
    rotated,
    joint,
    grad_out,
    totals,
    grad_nope,
    grad_rope,
    grad_joint,
    grad_key,
    bias,
):
    @pl.when(pl.program_id(0) == 0)
    def _():
        fill_bias(bias, row_here, row_across, first_across)
        grad_key[...] = jnp.zeros_like(grad_key)

    turn = turn_matrix(group * ROPE)
    rope_keys = key_rope[...]
    rope_keys_across = rope_keys.T
    rope_grads = []
    key_grad = jnp.zeros(grad_key.shape, FULL_TYPE)
    for head in range(group):
        keys = joint[:, head * 128 : head * 128 + NOPE]
        values = joint[:, head * 128 + NOPE : (head + 1) * 128]
        queries = query_nope[:, head * NOPE : (head + 1) * NOPE]
        turned = rotated[:, head * ROPE : (head + 1) * ROPE]
        out_grad = grad_out[:, head * VDIM : (head + 1) * VDIM]
        scores = (
            kernel_dot(keys, queries, NT) + kernel_dot(rope_keys, turned, NT)
        ) * SCORE_SCALE + bias[...]
        probs = jnp.exp(scores - totals[0, head : head + 1, :])
        value_grad = kernel_dot(probs.astype(HALF_TYPE), out_grad, NN)
        prob_grad = kernel_dot(values, out_grad, NT)
        delta = jnp.sum(probs * prob_grad, axis=0, keepdims=True)
        score_grad = (probs * (prob_grad - delta)).astype(HALF_TYPE)
        nope_key_grad = kernel_dot(score_grad, queries, NN) * SCORE_SCALE
        key_grad = key_grad + kernel_dot(score_grad, turned, NN)
        query_grad = kernel_dot(keys.T, score_grad, NN) * SCORE_SCALE
        rope_grads.append(kernel_dot(rope_keys_across, score_grad, NN))
        grad_nope[:, head * NOPE : (head + 1) * NOPE] = query_grad.T.astype(HALF_TYPE)
        grad_joint[:, head * 128 : head * 128 + NOPE] = nope_key_grad.astype(HALF_TYPE)
        grad_joint[:, head * 128 + NOPE : (head + 1) * 128] = value_grad.astype(HALF_TYPE)
    rope_grad = jnp.concatenate(rope_grads, axis=0).T * SCORE_SCALE
    grad_rope[...] = (
        rope_grad * cosine[...] + split_dot(rope_grad * sine[...], turn, NT)
    ).astype(HALF_TYPE)
    grad_key[...] += key_grad * SCORE_SCALE


def head_group(heads):
    return 4 if heads % 4 == 0 else heads


def attention_specs(tokens, group):
    whole = lambda *shape: pl.BlockSpec(shape, lambda step: (0,) * len(shape))
    wide = lambda width: pl.BlockSpec((tokens, width), lambda step: (0, step))
    shared = [
        whole(tokens, 1),
        whole(1, tokens),
        whole(1, tokens),
        whole(tokens, group * ROPE),
        whole(tokens, group * ROPE),
        whole(tokens, ROPE),
    ]
    totals = pl.BlockSpec((1, group, tokens), lambda step: (step, 0, 0))
    return (whole, wide, shared, totals)


def attention_forward(places, key_rope, query_nope, query_rope, joint, heads):
    tokens = joint.shape[0]
    group = head_group(heads)
    _, wide, shared, totals = attention_specs(tokens, group)
    return pl.pallas_call(
        functools.partial(attend_kernel, group),
        grid=(heads // group,),
        in_specs=shared + [wide(group * NOPE), wide(group * ROPE), wide(group * 128)],
        out_specs=[wide(group * VDIM), wide(group * ROPE), totals],
        out_shape=[
            jax.ShapeDtypeStruct((tokens, heads * VDIM), HALF_TYPE),
            jax.ShapeDtypeStruct((tokens, heads * ROPE), HALF_TYPE),
            jax.ShapeDtypeStruct((heads // group, group, tokens), FULL_TYPE),
        ],
        scratch_shapes=[pltpu.VMEM((tokens, tokens), FULL_TYPE)],
        compiler_params=pltpu.CompilerParams(vmem_limit_bytes=40 << 20),
        cost_estimate=pl.CostEstimate(
            flops=heads * tokens * tokens * 320,
            bytes_accessed=tokens * heads * 800,
            transcendentals=heads * tokens * tokens,
        ),
    )(*places, key_rope, query_nope, query_rope, joint)


def attention_backward(places, key_rope, query_nope, rotated, joint, grad_out, log_totals, heads):
    tokens = joint.shape[0]
    group = head_group(heads)
    whole, wide, shared, totals = attention_specs(tokens, group)
    return pl.pallas_call(
        functools.partial(attend_back_kernel, group),
        grid=(heads // group,),
        in_specs=shared
        + [wide(group * NOPE), wide(group * ROPE), wide(group * 128), wide(group * VDIM), totals],
        out_specs=[
            wide(group * NOPE),
            wide(group * ROPE),
            wide(group * 128),
            whole(tokens, ROPE),
        ],
        out_shape=[
            jax.ShapeDtypeStruct((tokens, heads * NOPE), HALF_TYPE),
            jax.ShapeDtypeStruct((tokens, heads * ROPE), HALF_TYPE),
            jax.ShapeDtypeStruct((tokens, heads * 128), HALF_TYPE),
            jax.ShapeDtypeStruct((tokens, ROPE), FULL_TYPE),
        ],
        scratch_shapes=[pltpu.VMEM((tokens, tokens), FULL_TYPE)],
        compiler_params=pltpu.CompilerParams(vmem_limit_bytes=40 << 20),
        cost_estimate=pl.CostEstimate(
            flops=heads * tokens * tokens * 900,
            bytes_accessed=tokens * heads * 1200,
            transcendentals=heads * tokens * tokens,
        ),
    )(*places, key_rope, query_nope, rotated, joint, grad_out, log_totals)


class Row:
    def __init__(self, size):
        self.size = size
        self.x_size = size // (Z_SIZE * CORES)
        index = lax.axis_index("row")
        self.z = index // (self.x_size * CORES)
        self.x = (index // CORES) % self.x_size
        self.core = index % CORES

    def move(self, values, dz=0, dx=0, dc=0):
        def at(z, x, c):
            return ((z % Z_SIZE) * self.x_size + x % self.x_size) * CORES + c % CORES

        pairs = [
            (at(z, x, c), at(z + dz, x + dx, c + dc))
            for z in range(Z_SIZE)
            for x in range(self.x_size)
            for c in range(CORES)
        ]
        return lax.ppermute(values, "row", pairs)

    def quarter(self, array, dx, dc):
        blocks = array.reshape(
            (Z_SIZE, self.x_size, CORES, array.shape[0] // self.size, array.shape[1])
        )
        x_at = lax.rem(self.x + dx, self.x_size)
        core_at = lax.rem(self.core + dc, CORES)
        part = lax.dynamic_slice(
            blocks,
            (0, x_at, core_at, 0, 0),
            (Z_SIZE, 1, 1) + blocks.shape[3:],
        )
        return part.reshape((-1, array.shape[1]))

    def reduce_scatter(self, piece):
        def over_cores(dx):
            other = self.move(piece(dx, 1).astype(HALF_TYPE), dc=1)
            return piece(dx, 0) + other.astype(FULL_TYPE)

        total = over_cores(self.x_size - 1).astype(HALF_TYPE)
        for step in range(1, self.x_size):
            came = self.move(total, dx=1)
            mine = over_cores(self.x_size - 1 - step)
            total = (came.astype(FULL_TYPE) + mine).astype(HALF_TYPE)
        blocks = total.reshape((Z_SIZE, -1, total.shape[1]))

        def block(dz):
            return lax.dynamic_index_in_dim(
                blocks, lax.rem(self.z + dz, Z_SIZE), 0, keepdims=False
            )

        total = block(Z_SIZE - 1)
        for step in range(1, Z_SIZE):
            came = self.move(total, dz=1)
            total = came.astype(FULL_TYPE) + block(Z_SIZE - 1 - step).astype(FULL_TYPE)
            if step < Z_SIZE - 1:
                total = total.astype(HALF_TYPE)
        return total


def col_gather(values, col_count):
    if col_count != 2:
        return lax.all_gather(values, "col", axis=1, tiled=True)
    other = lax.ppermute(values, "col", [(0, 1), (1, 0)])
    first = lax.axis_index("col") == 0
    return jnp.concatenate(
        [jnp.where(first, values, other), jnp.where(first, other, values)], axis=1
    )


def col_sum(values, col_count):
    half = values.astype(HALF_TYPE)
    if col_count != 2:
        return lax.psum(half.astype(FULL_TYPE), "col")
    other = lax.ppermute(half, "col", [(0, 1), (1, 0)])
    return half.astype(FULL_TYPE) + other.astype(FULL_TYPE)


def heads_apart(weight, heads):
    split = weight.reshape(weight.shape[0], heads, NOPE + ROPE)
    return jnp.concatenate(
        [
            split[:, :, :NOPE].reshape(weight.shape[0], heads * NOPE),
            split[:, :, NOPE:].reshape(weight.shape[0], heads * ROPE),
        ],
        axis=1,
    )


def heads_together(weight, heads):
    rows = weight.shape[0]
    return jnp.concatenate(
        [
            weight[:, : heads * NOPE].reshape(rows, heads, NOPE),
            weight[:, heads * NOPE :].reshape(rows, heads, ROPE),
        ],
        axis=2,
    ).reshape(rows, heads * (NOPE + ROPE))


def fold_count(height, width, rows):
    count = rows // height
    while width % count:
        count -= 1
    return count


def fold_up(weight, devices, rows):
    height = weight.shape[0] // devices
    count = fold_count(height, weight.shape[1], rows)
    width = weight.shape[1] // count
    folded = jnp.swapaxes(weight.reshape(devices, height, count, width), 1, 2)
    folded = folded.reshape(devices, count * height, width)
    folded = jnp.pad(folded, ((0, 0), (0, rows - count * height), (0, 0)))
    return folded.reshape(devices * rows, width)


def unfold(folded, devices, height, width):
    rows = folded.shape[0] // devices
    count = fold_count(height, width, rows)
    blocks = folded.reshape(devices, rows, folded.shape[1])[:, : count * height]
    blocks = blocks.reshape(devices, count, height, folded.shape[1])
    return jnp.swapaxes(blocks, 1, 2).reshape(devices * height, width)


GAIN_LANES = 32


def fold_gains(gains, devices, rows):
    flat = gains.reshape(devices, -1)
    short = -flat.shape[1] % GAIN_LANES
    flat = jnp.pad(flat, ((0, 0), (0, short)))
    blocks = flat.reshape(devices, -1, GAIN_LANES)
    blocks = jnp.pad(blocks, ((0, 0), (0, rows - blocks.shape[1]), (0, 0)))
    return blocks.reshape(devices * rows, GAIN_LANES)


def unfold_gains(folded, devices, count):
    flat = folded.reshape(devices, -1)
    return flat[:, :count].reshape(-1)


def body(
    tokens,
    dest_row,
    seq_lens,
    cotangent,
    query_down,
    joint_down,
    query_up,
    joint_up,
    out_weight,
    gate_weight,
    up_weight,
    down_weight,
    norm_gains,
    first_query_down,
    first_joint_down,
    first_query_up,
    first_joint_up,
    first_out_weight,
    first_gate_weight,
    first_up_weight,
    first_down_weight,
    first_norm_gains,
    second_query_down,
    second_joint_down,
    second_query_up,
    second_joint_up,
    second_out_weight,
    second_gate_weight,
    second_up_weight,
    second_down_weight,
    second_norm_gains,
):
    params = (
        query_down,
        joint_down,
        query_up,
        joint_up,
        out_weight,
        gate_weight,
        up_weight,
        down_weight,
        norm_gains,
    )
    firsts = (
        first_query_down,
        first_joint_down,
        first_query_up,
        first_joint_up,
        first_out_weight,
        first_gate_weight,
        first_up_weight,
        first_down_weight,
        first_norm_gains,
    )
    seconds = (
        second_query_down,
        second_joint_down,
        second_query_up,
        second_joint_up,
        second_out_weight,
        second_gate_weight,
        second_up_weight,
        second_down_weight,
        second_norm_gains,
    )
    col_count = lax.axis_size("col")
    col_index = lax.axis_index("col")
    row_count = lax.axis_size("row")
    row = Row(row_count)
    heads = HEADS // col_count
    width_share = D // col_count
    token_count = tokens.shape[0]
    col_start = col_index * width_share
    shard_rows = query_down.shape[0]
    gain_count = norm_gains.shape[0]
    ffn_width = gate_weight.shape[1]

    half = lambda weight: weight.astype(HALF_TYPE)
    parts = [
        half(query_down),
        half(out_weight),
        fold_up(half(joint_up), 1, shard_rows),
        fold_up(heads_apart(half(query_up), heads), 1, shard_rows),
        half(joint_down),
        fold_gains(half(norm_gains), 1, shard_rows),
    ]
    offsets = [0]
    for part in parts:
        offsets.append(offsets[-1] + part.shape[1])
    spare = -offsets[-1] % 128
    packed_one = jnp.concatenate(
        parts + [jnp.zeros((shard_rows, spare), HALF_TYPE), half(gate_weight)], axis=1
    )
    packed_two = jnp.concatenate([half(up_weight), half(down_weight)], axis=1)
    gathered_one = lax.all_gather(packed_one, "row", axis=0, tiled=True)
    gathered_two = lax.all_gather(packed_two, "row", axis=0, tiled=True)
    taken = [gathered_one[:, offsets[i] : offsets[i + 1]] for i in range(6)]
    query_down_all = taken[0]
    out_all = taken[1]
    joint_up_all = unfold(taken[2], row_count, joint_up.shape[0], joint_up.shape[1])
    query_up_all = unfold(taken[3], row_count, query_up.shape[0], query_up.shape[1])
    joint_down_all = taken[4]
    gains_all = unfold_gains(taken[5], row_count, gain_count).astype(FULL_TYPE)
    gate_all = gathered_one[:, offsets[-1] + spare :]
    up_all = gathered_two[:, :ffn_width]
    down_all = gathered_two[:, ffn_width:]
    gain_one = gains_all[:D]
    gain_two = gains_all[D : 2 * D]
    gain_query = gains_all[2 * D : 2 * D + Q_RANK]
    gain_joint = gains_all[2 * D + Q_RANK :]
    query_nope_all = query_up_all[:, : heads * NOPE]
    query_rope_all = query_up_all[:, heads * NOPE :]

    share = token_count // row_count
    target = dest_row // CAP
    local_rows = dest_row - target * CAP
    ids = jnp.arange(token_count, dtype=jnp.int32)
    same_before = (target[:, None] == target[None, :]) & (ids[None, :] < ids[:, None])
    slots = target * share + jnp.sum(same_before.astype(jnp.int32), axis=1)
    sends = slots[None, :] == ids[:, None]
    send_matrix = sends.astype(HALF_TYPE)
    sorted_rows = jnp.sum(jnp.where(sends, local_rows[None, :], 0), axis=1)
    sorted_tokens = product(send_matrix, tokens).astype(HALF_TYPE)
    arrived_rows = lax.all_to_all(
        sorted_rows, "row", split_axis=0, concat_axis=0, tiled=True
    )
    arrived = lax.all_to_all(sorted_tokens, "row", split_axis=0, concat_axis=0, tiled=True)

    lengths = seq_lens[0]
    padded = (lengths + BLK - 1) // BLK * BLK
    endings = CAP - jnp.sum(padded) + jnp.cumsum(padded)
    starts = endings - lengths
    inside = (arrived_rows[:, None] >= starts[None, :]) & (
        arrived_rows[:, None] < endings[None, :]
    )
    first_rows = jnp.sum(jnp.where(inside, starts[None, :], 0), axis=1)
    position = (arrived_rows - first_rows).astype(FULL_TYPE)
    frequency = 10000.0 ** (-(jnp.arange(ROPE // 2, dtype=FULL_TYPE) * 2.0 / ROPE))
    angles = position[:, None] * frequency[None, :]
    cosine = jnp.tile(jnp.cos(angles), (1, 2))
    sine = jnp.tile(jnp.sin(angles), (1, 2))
    group = head_group(heads)
    places = (
        arrived_rows[:, None],
        arrived_rows[None, :],
        first_rows[None, :],
        jnp.tile(cosine, (1, group)),
        jnp.tile(sine, (1, group)),
    )
    row_matrix = (
        jnp.arange(CAP, dtype=jnp.int32)[:, None] == arrived_rows[None, :]
    ).astype(HALF_TYPE)
    upstream_part = contract_rows(row_matrix, cotangent).astype(HALF_TYPE)

    features = col_gather(arrived, col_count)
    upstream = col_gather(upstream_part, col_count).astype(FULL_TYPE)
    ffn_grad = (RESIDUAL_SCALE * upstream).astype(HALF_TYPE)

    inputs = features.astype(FULL_TYPE)
    scale_one = rms_scale(inputs)
    normed_one = (inputs * scale_one * gain_one).astype(HALF_TYPE)
    query_latent = product(normed_one, query_down_all)
    joint_latent = product(normed_one, joint_down_all)
    scale_query = rms_scale(query_latent)
    query_normed = (query_latent * scale_query * gain_query).astype(HALF_TYPE)
    compressed_raw = joint_latent[:, :KV_RANK]
    scale_joint = rms_scale(compressed_raw)
    compressed = (compressed_raw * scale_joint * gain_joint).astype(HALF_TYPE)
    rope_raw = joint_latent[:, KV_RANK:]
    key_rope = (rope_raw * cosine + rotate_half(rope_raw) * sine).astype(HALF_TYPE)
    query_nope = product(query_normed, query_nope_all).astype(HALF_TYPE)
    query_rope = product(query_normed, query_rope_all)
    joint_full = product(compressed, joint_up_all).astype(HALF_TYPE)
    attended, rotated, log_totals = attention_forward(
        places, key_rope, query_nope, query_rope, joint_full, heads
    )
    branch = col_sum(times_transposed(attended, out_all), col_count)
    residual = inputs + RESIDUAL_SCALE * branch

    scale_two = rms_scale(residual)
    normed_two = (residual * scale_two * gain_two).astype(HALF_TYPE)
    gate_rows = product(normed_two, gate_all)
    up_rows = product(normed_two, up_all)
    sigmoid_gate = jax.nn.sigmoid(gate_rows)
    activated = (gate_rows * sigmoid_gate * up_rows).astype(HALF_TYPE)
    ffn_grad_across = ffn_grad.T
    normed_two_across = normed_two.T
    normed_one_across = normed_one.T

    def from_rows(across, right_side):
        return lambda dx, dc: product(row.quarter(across, dx, dc), right_side)

    down_grad = row.reduce_scatter(from_rows(ffn_grad_across, activated))
    grad_act = product(ffn_grad, down_all)
    grad_gate = (
        grad_act * up_rows * sigmoid_gate * (1.0 + gate_rows * (1.0 - sigmoid_gate))
    ).astype(HALF_TYPE)
    grad_up = (grad_act * gate_rows * sigmoid_gate).astype(HALF_TYPE)
    gate_grad = row.reduce_scatter(from_rows(normed_two_across, grad_gate))
    up_grad = row.reduce_scatter(from_rows(normed_two_across, grad_up))

    feed_forward = times_transposed(activated, down_all)
    feed_forward = lax.psum_scatter(
        feed_forward.astype(HALF_TYPE), "col", scatter_dimension=1, tiled=True
    ).astype(FULL_TYPE)
    residual_part = lax.dynamic_slice_in_dim(residual, col_start, width_share, 1)
    output_rows = residual_part + RESIDUAL_SCALE * feed_forward
    output_pad = product(row_matrix, output_rows.astype(HALF_TYPE)).astype(HALF_TYPE)

    grad_normed_two = col_sum(
        times_transposed(grad_gate, gate_all) + times_transposed(grad_up, up_all), col_count
    )
    through_two, gain_two_grad = rms_backward(grad_normed_two, residual, scale_two, gain_two)
    grad_residual = upstream + through_two
    branch_grad = (RESIDUAL_SCALE * grad_residual).astype(HALF_TYPE)
    out_grad = row.reduce_scatter(from_rows(branch_grad.T, attended))
    grad_attended = product(branch_grad, out_all).astype(HALF_TYPE)

    grad_nope, grad_rope, grad_joint_full, grad_key = attention_backward(
        places, key_rope, query_nope, rotated, joint_full, grad_attended, log_totals, heads
    )
    query_up_grad = jnp.concatenate(
        [contract_rows(query_normed, grad_nope), contract_rows(query_normed, grad_rope)], axis=1
    )
    joint_up_grad = contract_rows(compressed, grad_joint_full)
    folded_grads = jnp.concatenate(
        [
            fold_up(query_up_grad.astype(HALF_TYPE), row_count, shard_rows),
            fold_up(joint_up_grad.astype(HALF_TYPE), row_count, shard_rows),
        ],
        axis=1,
    )
    heads_grad = row.reduce_scatter(
        lambda dx, dc: row.quarter(folded_grads, dx, dc).astype(FULL_TYPE)
    )
    latents = col_sum(
        jnp.concatenate(
            [
                times_transposed(grad_nope, query_nope_all)
                + times_transposed(grad_rope, query_rope_all),
                times_transposed(grad_joint_full, joint_up_all),
                grad_key,
            ],
            axis=1,
        ),
        col_count,
    )
    grad_query_normed = latents[:, :Q_RANK]
    grad_compressed = latents[:, Q_RANK : Q_RANK + KV_RANK]
    grad_rope_sum = latents[:, Q_RANK + KV_RANK :]
    grad_query_latent, gain_query_grad = rms_backward(
        grad_query_normed, query_latent, scale_query, gain_query
    )
    grad_compressed_raw, gain_joint_grad = rms_backward(
        grad_compressed, compressed_raw, scale_joint, gain_joint
    )
    grad_key_raw = grad_rope_sum * cosine + rotate_back(grad_rope_sum * sine)
    grad_latents = jnp.concatenate(
        [grad_query_latent, grad_compressed_raw, grad_key_raw], axis=1
    ).astype(HALF_TYPE)
    grad_normed_one = times_transposed(
        grad_latents[:, :Q_RANK], query_down_all
    ) + times_transposed(grad_latents[:, Q_RANK:], joint_down_all)
    through_one, gain_one_grad = rms_backward(grad_normed_one, inputs, scale_one, gain_one)
    grad_inputs = lax.dynamic_slice_in_dim(
        grad_residual + through_one, col_start, width_share, 1
    ).astype(HALF_TYPE)
    returned = lax.all_to_all(grad_inputs, "row", split_axis=0, concat_axis=0, tiled=True)
    grad_tokens = contract_rows(send_matrix, returned).astype(HALF_TYPE)
    gains_grad = fold_gains(
        jnp.concatenate([gain_one_grad, gain_two_grad, gain_query_grad, gain_joint_grad]),
        row_count,
        shard_rows,
    )
    downs_grad = row.reduce_scatter(
        lambda dx, dc: jnp.concatenate(
            [
                product(row.quarter(normed_one_across, dx, dc), grad_latents),
                row.quarter(gains_grad, dx, dc),
            ],
            axis=1,
        )
    )
    query_fold = taken[3].shape[1]
    reduced = (
        downs_grad[:, :Q_RANK],
        downs_grad[:, Q_RANK : Q_RANK + KV_RANK + ROPE],
        heads_together(
            unfold(heads_grad[:, :query_fold], 1, query_up.shape[0], query_up.shape[1]), heads
        ),
        unfold(heads_grad[:, query_fold:], 1, joint_up.shape[0], joint_up.shape[1]),
        out_grad,
        gate_grad,
        up_grad,
        down_grad,
        unfold_gains(downs_grad[:, Q_RANK + KV_RANK + ROPE :], 1, gain_count),
    )
    step_rates = learning_rates()
    seconds_next = []
    weights_next = []
    for slot_index in range(9):
        second_new, weight_new = adam_update(
            params[slot_index],
            reduced[slot_index],
            firsts[slot_index],
            seconds[slot_index],
            step_rates[slot_index],
        )
        seconds_next.append(second_new)
        weights_next.append(weight_new)
    return (output_pad, grad_tokens) + reduced + tuple(seconds_next) + tuple(weights_next)


def solution(mesh):
    in_specs = (
        P("row", "col"),
        P("row"),
        P("row", None),
        P("row", "col"),
        P("row", None),
        P("row", None),
        P("row", "col"),
        P("row", "col"),
        P("row", "col"),
        P("row", "col"),
        P("row", "col"),
        P("row", "col"),
        P("row"),
        P("row", None),
        P("row", None),
        P("row", "col"),
        P("row", "col"),
        P("row", "col"),
        P("row", "col"),
        P("row", "col"),
        P("row", "col"),
        P("row"),
        P("row", None),
        P("row", None),
        P("row", "col"),
        P("row", "col"),
        P("row", "col"),
        P("row", "col"),
        P("row", "col"),
        P("row", "col"),
        P("row"),
    )
    out_specs = (
        P("row", "col"),
        P("row", "col"),
        P("row", None),
        P("row", None),
        P("row", "col"),
        P("row", "col"),
        P("row", "col"),
        P("row", "col"),
        P("row", "col"),
        P("row", "col"),
        P("row"),
        P("row", None),
        P("row", None),
        P("row", "col"),
        P("row", "col"),
        P("row", "col"),
        P("row", "col"),
        P("row", "col"),
        P("row", "col"),
        P("row"),
        P("row", None),
        P("row", None),
        P("row", "col"),
        P("row", "col"),
        P("row", "col"),
        P("row", "col"),
        P("row", "col"),
        P("row", "col"),
        P("row"),
    )
    return jax.shard_map(body, mesh=mesh, in_specs=in_specs, out_specs=out_specs, check_vma=False)
```

```python
import functools

import jax
import jax.numpy as jnp
from jax import lax
from jax.experimental import pallas as pl
from jax.experimental.pallas import tpu as pltpu
from jax.sharding import PartitionSpec as P

D = 2560
FF = 6400
HEADS = 40
NOPE = 64
ROPE = 32
VDIM = 64
Q_RANK = 768
KV_RANK = 256
SEQS = 4
BLK = 128
STEP = 10
CAP = 896

Z_SIZE = 4
CORES = 2

EPSILON = 1e-05
RESIDUAL_SCALE = 1.4 / 62**0.5
BETA_ONE = 0.9
BETA_TWO = 0.95
ADAM_EPSILON = 1e-08
DECAY_RATE = 0.1
MASKED = -1e30
SCORE_SCALE = (NOPE + ROPE) ** (-0.5)
FULL_TYPE = jnp.float32
HALF_TYPE = jnp.bfloat16


def rms_scale(values):
    return lax.rsqrt(jnp.mean(values * values, axis=-1, keepdims=True) + EPSILON)


def rms_backward(grad_normed, values, norm_scale, gain_values):
    weighted = grad_normed * gain_values
    mean_term = jnp.mean(weighted * values, axis=-1, keepdims=True)
    grad_values = norm_scale * weighted - values * norm_scale**3 * mean_term
    grad_gain = jnp.sum(grad_normed * values * norm_scale, axis=0)
    return (grad_values, grad_gain)


def product(left_side, right_side):
    return jnp.dot(left_side, right_side, preferred_element_type=FULL_TYPE)


def contract_rows(left_side, right_side):
    return lax.dot_general(
        left_side, right_side, (((0,), (0,)), ((), ())), preferred_element_type=FULL_TYPE
    )


def times_transposed(left_side, right_side):
    return lax.dot_general(
        left_side, right_side, (((1,), (1,)), ((), ())), preferred_element_type=FULL_TYPE
    )


def rotate_half(values):
    half_width = values.shape[-1] // 2
    return jnp.concatenate([-values[..., half_width:], values[..., :half_width]], axis=-1)


def rotate_back(values):
    half_width = values.shape[-1] // 2
    return jnp.concatenate([values[..., half_width:], -values[..., :half_width]], axis=-1)


def learning_rates():
    return (
        3.0 * D ** (-0.5),
        3.0 * D ** (-0.5),
        3.0 * (Q_RANK // 2) ** (-0.5),
        3.0 * KV_RANK ** (-0.5),
        3.0 * max(HEADS * VDIM // 512, 1) ** (-0.5),
        3.0 * D ** (-0.5),
        3.0 * D ** (-0.5),
        3.0 * max(FF // 80, 1) ** (-0.5),
        0.6,
    )


def adam_update(weight_old, grad_value, first_old, second_old, step_rate):
    first_new = BETA_ONE * first_old + (1.0 - BETA_ONE) * grad_value
    second_new = BETA_TWO * second_old + (1.0 - BETA_TWO) * grad_value * grad_value
    first_hat = first_new / (1.0 - BETA_ONE**STEP)
    second_hat = second_new / (1.0 - BETA_TWO**STEP)
    weight_new = weight_old - step_rate * (
        first_hat / (jnp.sqrt(second_hat) + ADAM_EPSILON) + DECAY_RATE * weight_old
    )
    return (second_new, weight_new)


def turn_matrix(width):
    rows = lax.broadcasted_iota(jnp.int32, (width, width), 0)
    columns = lax.broadcasted_iota(jnp.int32, (width, width), 1)
    half = ROPE // 2
    in_first = (columns % ROPE) < half
    minus = in_first & (rows == columns + half)
    plus = jnp.logical_not(in_first) & (rows == columns - half)
    return jnp.where(plus, 1.0, jnp.where(minus, -1.0, 0.0)).astype(HALF_TYPE)


def split_dot(values, matrix, dims):
    high = values.astype(HALF_TYPE)
    low = (values - high.astype(FULL_TYPE)).astype(HALF_TYPE)
    dot = functools.partial(
        lax.dot_general, dimension_numbers=(dims, ((), ())), preferred_element_type=FULL_TYPE
    )
    return dot(high, matrix) + dot(low, matrix)


NT = ((1,), (1,))
NN = ((1,), (0,))


def kernel_dot(left_side, right_side, dims):
    return lax.dot_general(
        left_side, right_side, (dims, ((), ())), preferred_element_type=FULL_TYPE
    )


def fill_bias(bias_ref, row_here, row_across, first_across):
    key_rows = row_here[...]
    allowed = (key_rows >= first_across[...]) & (key_rows <= row_across[...])
    bias_ref[...] = jnp.where(allowed, 0.0, MASKED)


def attend_kernel(
    group,
    row_here,
    row_across,
    first_across,
    cosine,
    sine,
    key_rope,
    query_nope,
    query_rope,
    joint,
    attended,
    rotated,
    totals,
    bias,
):
    @pl.when(pl.program_id(0) == 0)
    def _():
        fill_bias(bias, row_here, row_across, first_across)

    turn = turn_matrix(group * ROPE)
    rope_in = query_rope[...]
    rotated[...] = (
        rope_in * cosine[...] + split_dot(rope_in, turn, NN) * sine[...]
    ).astype(HALF_TYPE)
    rope_keys = key_rope[...]
    for head in range(group):
        keys = joint[:, head * 128 : head * 128 + NOPE]
        values = joint[:, head * 128 + NOPE : (head + 1) * 128]
        scores = (
            kernel_dot(keys, query_nope[:, head * NOPE : (head + 1) * NOPE], NT)
            + kernel_dot(rope_keys, rotated[:, head * ROPE : (head + 1) * ROPE], NT)
        ) * SCORE_SCALE + bias[...]
        top = jnp.max(scores, axis=0, keepdims=True)
        powers = jnp.exp(scores - top)
        total = jnp.sum(powers, axis=0, keepdims=True)
        weights = (powers * (1.0 / total)).astype(HALF_TYPE)
        found = kernel_dot(values.T, weights, NN)
        attended[:, head * VDIM : (head + 1) * VDIM] = found.T.astype(HALF_TYPE)
        totals[0, head : head + 1, :] = top + jnp.log(total)


def attend_back_kernel(
    group,
    row_here,
    row_across,
    first_across,
    cosine,
    sine,
    key_rope,
    query_nope,
    rotated,
    joint,
    grad_out,
    totals,
    grad_nope,
    grad_rope,
    grad_joint,
    grad_key,
    bias,
):
    @pl.when(pl.program_id(0) == 0)
    def _():
        fill_bias(bias, row_here, row_across, first_across)
        grad_key[...] = jnp.zeros_like(grad_key)

    turn = turn_matrix(group * ROPE)
    rope_keys = key_rope[...]
    rope_keys_across = rope_keys.T
    rope_grads = []
    key_grad = jnp.zeros(grad_key.shape, FULL_TYPE)
    for head in range(group):
        keys = joint[:, head * 128 : head * 128 + NOPE]
        values = joint[:, head * 128 + NOPE : (head + 1) * 128]
        queries = query_nope[:, head * NOPE : (head + 1) * NOPE]
        turned = rotated[:, head * ROPE : (head + 1) * ROPE]
        out_grad = grad_out[:, head * VDIM : (head + 1) * VDIM]
        scores = (
            kernel_dot(keys, queries, NT) + kernel_dot(rope_keys, turned, NT)
        ) * SCORE_SCALE + bias[...]
        probs = jnp.exp(scores - totals[0, head : head + 1, :])
        value_grad = kernel_dot(probs.astype(HALF_TYPE), out_grad, NN)
        prob_grad = kernel_dot(values, out_grad, NT)
        delta = jnp.sum(probs * prob_grad, axis=0, keepdims=True)
        score_grad = (probs * (prob_grad - delta)).astype(HALF_TYPE)
        nope_key_grad = kernel_dot(score_grad, queries, NN) * SCORE_SCALE
        key_grad = key_grad + kernel_dot(score_grad, turned, NN)
        query_grad = kernel_dot(keys.T, score_grad, NN) * SCORE_SCALE
        rope_grads.append(kernel_dot(rope_keys_across, score_grad, NN))
        grad_nope[:, head * NOPE : (head + 1) * NOPE] = query_grad.T.astype(HALF_TYPE)
        grad_joint[:, head * 128 : head * 128 + NOPE] = nope_key_grad.astype(HALF_TYPE)
        grad_joint[:, head * 128 + NOPE : (head + 1) * 128] = value_grad.astype(HALF_TYPE)
    rope_grad = jnp.concatenate(rope_grads, axis=0).T * SCORE_SCALE
    grad_rope[...] = (
        rope_grad * cosine[...] + split_dot(rope_grad * sine[...], turn, NT)
    ).astype(HALF_TYPE)
    grad_key[...] += key_grad * SCORE_SCALE


def head_group(heads):
    return 4 if heads % 4 == 0 else heads


def attention_specs(tokens, group):
    whole = lambda *shape: pl.BlockSpec(shape, lambda step: (0,) * len(shape))
    wide = lambda width: pl.BlockSpec((tokens, width), lambda step: (0, step))
    shared = [
        whole(tokens, 1),
        whole(1, tokens),
        whole(1, tokens),
        whole(tokens, group * ROPE),
        whole(tokens, group * ROPE),
        whole(tokens, ROPE),
    ]
    totals = pl.BlockSpec((1, group, tokens), lambda step: (step, 0, 0))
    return (whole, wide, shared, totals)


def attention_forward(places, key_rope, query_nope, query_rope, joint, heads):
    tokens = joint.shape[0]
    group = head_group(heads)
    _, wide, shared, totals = attention_specs(tokens, group)
    return pl.pallas_call(
        functools.partial(attend_kernel, group),
        grid=(heads // group,),
        in_specs=shared + [wide(group * NOPE), wide(group * ROPE), wide(group * 128)],
        out_specs=[wide(group * VDIM), wide(group * ROPE), totals],
        out_shape=[
            jax.ShapeDtypeStruct((tokens, heads * VDIM), HALF_TYPE),
            jax.ShapeDtypeStruct((tokens, heads * ROPE), HALF_TYPE),
            jax.ShapeDtypeStruct((heads // group, group, tokens), FULL_TYPE),
        ],
        scratch_shapes=[pltpu.VMEM((tokens, tokens), FULL_TYPE)],
        compiler_params=pltpu.CompilerParams(vmem_limit_bytes=40 << 20),
        cost_estimate=hint(),
    )(*places, key_rope, query_nope, query_rope, joint)


def attention_backward(places, key_rope, query_nope, rotated, joint, grad_out, log_totals, heads):
    tokens = joint.shape[0]
    group = head_group(heads)
    whole, wide, shared, totals = attention_specs(tokens, group)
    return pl.pallas_call(
        functools.partial(attend_back_kernel, group),
        grid=(heads // group,),
        in_specs=shared
        + [wide(group * NOPE), wide(group * ROPE), wide(group * 128), wide(group * VDIM), totals],
        out_specs=[
            wide(group * NOPE),
            wide(group * ROPE),
            wide(group * 128),
            whole(tokens, ROPE),
        ],
        out_shape=[
            jax.ShapeDtypeStruct((tokens, heads * NOPE), HALF_TYPE),
            jax.ShapeDtypeStruct((tokens, heads * ROPE), HALF_TYPE),
            jax.ShapeDtypeStruct((tokens, heads * 128), HALF_TYPE),
            jax.ShapeDtypeStruct((tokens, ROPE), FULL_TYPE),
        ],
        scratch_shapes=[pltpu.VMEM((tokens, tokens), FULL_TYPE)],
        compiler_params=pltpu.CompilerParams(vmem_limit_bytes=40 << 20),
        cost_estimate=hint(),
    )(*places, key_rope, query_nope, rotated, joint, grad_out, log_totals)


LANES = 128
KERNEL_MEMORY = 58 << 20


def tile_of(width, most):
    return max(
        (tile for tile in range(LANES, most + 1, LANES) if width % tile == 0), default=None
    )


def hint():
    return pl.CostEstimate(flops=1, bytes_accessed=1, transcendentals=0)


def feed_terms(gate_rows, up_rows, grad_act):
    sigmoid_gate = 1.0 / (1.0 + jnp.exp(-gate_rows))
    silu = gate_rows * sigmoid_gate
    activated = silu * up_rows
    grad_gate = grad_act * up_rows * sigmoid_gate * (1.0 + gate_rows * (1.0 - sigmoid_gate))
    return [value.astype(HALF_TYPE) for value in (activated, grad_gate, grad_act * silu)]


def feed_kernel(normed, ffn_grad, gate, up, down, activated, grad_gate, grad_up):
    gate_rows = kernel_dot(normed[...], gate[...], NN)
    up_rows = kernel_dot(normed[...], up[...], NN)
    grad_act = kernel_dot(ffn_grad[...], down[...], NN)
    activated[...], grad_gate[...], grad_up[...] = feed_terms(gate_rows, up_rows, grad_act)


def feed_part(normed, ffn_grad, gathered, width):
    tokens, depth = normed.shape
    tile = tile_of(width, 512)
    if tile is None:
        gate, up, down = [gathered[:, index * width : (index + 1) * width] for index in range(3)]
        return feed_terms(product(normed, gate), product(normed, up), product(ffn_grad, down))
    count = width // tile
    whole = pl.BlockSpec((tokens, depth), lambda step: (0, 0))
    part = lambda index: pl.BlockSpec((depth, tile), lambda step: (0, index * count + step))
    return pl.pallas_call(
        feed_kernel,
        grid=(count,),
        in_specs=[whole, whole, part(0), part(1), part(2)],
        out_specs=[pl.BlockSpec((tokens, tile), lambda step: (0, step))] * 3,
        out_shape=[jax.ShapeDtypeStruct((tokens, width), HALF_TYPE)] * 3,
        compiler_params=pltpu.CompilerParams(vmem_limit_bytes=KERNEL_MEMORY),
        cost_estimate=hint(),
    )(normed, ffn_grad, gathered, gathered, gathered)


def across_kernel(count, *refs):
    total = kernel_dot(refs[0][...], refs[count][...], NT)
    for index in range(1, count):
        total = total + kernel_dot(refs[index][...], refs[count + index][...], NT)
    for more in refs[2 * count : -1]:
        total = total + more[...]
    refs[-1][...] = total.astype(refs[-1].dtype)


def across_part(sides, places, gathered, earlier, kind):
    tokens, width = sides[0].shape
    depth = gathered.shape[0]
    if width % LANES:
        total = sum(
            times_transposed(side, gathered[:, place * width : (place + 1) * width])
            for side, place in zip(sides, places, strict=True)
        )
        return sum(earlier, total).astype(kind)
    tile = tile_of(depth, 512)
    block = pl.BlockSpec((tokens, tile), lambda step: (0, step))
    rows = lambda place: pl.BlockSpec((tile, width), lambda step: (step, place))
    return pl.pallas_call(
        functools.partial(across_kernel, len(sides)),
        grid=(depth // tile,),
        in_specs=[pl.BlockSpec((tokens, width), lambda step: (0, 0))] * len(sides)
        + [rows(place) for place in places]
        + [block] * len(earlier),
        out_specs=block,
        out_shape=jax.ShapeDtypeStruct((tokens, depth), kind),
        compiler_params=pltpu.CompilerParams(vmem_limit_bytes=KERNEL_MEMORY),
        cost_estimate=hint(),
    )(*sides, *[gathered] * len(sides), *earlier)


def piece_kernel(places, left_side, right_side, *refs):
    rows = left_side[...].reshape(-1, left_side.shape[-1])
    total = kernel_dot(rows, right_side[...], NN)
    for more in refs[:-1]:
        total = total + more[...].astype(FULL_TYPE)
    refs[-1][...] = total.astype(HALF_TYPE)


def piece_product(blocks, x_at, core_at, right_side, earlier):
    z_size, _, _, rows, tokens = blocks.shape
    width = right_side.shape[1]
    tile = tile_of(width, 1280)
    if tile is None or rows % 16:
        left_side = lax.dynamic_slice(
            blocks, (0, x_at, core_at, 0, 0), (z_size, 1, 1, rows, tokens)
        )
        total = product(left_side.reshape(-1, tokens), right_side)
        return sum([more.astype(FULL_TYPE) for more in earlier], total).astype(HALF_TYPE)
    block = pl.BlockSpec((z_size * rows, tile), lambda step, places: (0, step))
    return pl.pallas_call(
        piece_kernel,
        grid_spec=pltpu.PrefetchScalarGridSpec(
            num_scalar_prefetch=1,
            grid=(width // tile,),
            in_specs=[
                pl.BlockSpec(
                    (z_size, 1, 1, rows, tokens),
                    lambda step, places: (0, places[0], places[1], 0, 0),
                ),
                pl.BlockSpec((tokens, tile), lambda step, places: (0, step)),
            ]
            + [block] * len(earlier),
            out_specs=block,
        ),
        out_shape=jax.ShapeDtypeStruct((z_size * rows, width), HALF_TYPE),
        compiler_params=pltpu.CompilerParams(vmem_limit_bytes=KERNEL_MEMORY),
        cost_estimate=hint(),
    )(jnp.stack([x_at, core_at]).astype(jnp.int32), blocks, right_side, *earlier)


class Row:
    def __init__(self, size):
        self.size = size
        self.x_size = size // (Z_SIZE * CORES)
        index = lax.axis_index("row")
        self.z = index // (self.x_size * CORES)
        self.x = (index // CORES) % self.x_size
        self.core = index % CORES
        self.x_link = Link(functools.partial(self.move, dx=1))

    def move(self, values, dz=0, dx=0, dc=0):
        def at(z, x, c):
            return ((z % Z_SIZE) * self.x_size + x % self.x_size) * CORES + c % CORES

        pairs = [
            (at(z, x, c), at(z + dz, x + dx, c + dc))
            for z in range(Z_SIZE)
            for x in range(self.x_size)
            for c in range(CORES)
        ]
        return lax.ppermute(values, "row", pairs)

    def quarter(self, array, dx, dc):
        blocks = array.reshape(
            (Z_SIZE, self.x_size, CORES, array.shape[0] // self.size, array.shape[1])
        )
        x_at = lax.rem(self.x + dx, self.x_size)
        core_at = lax.rem(self.core + dc, CORES)
        part = lax.dynamic_slice(
            blocks,
            (0, x_at, core_at, 0, 0),
            (Z_SIZE, 1, 1) + blocks.shape[3:],
        )
        return part.reshape((-1, array.shape[1]))

    def halves(self, array, dc):
        blocks = array.reshape(
            (Z_SIZE * self.x_size, CORES, array.shape[0] // self.size, array.shape[1])
        )
        part = lax.dynamic_slice_in_dim(blocks, lax.rem(self.core + dc, CORES), 1, 1)
        return part.reshape((-1, array.shape[1]))

    def over_cores(self, terms):
        other = self.move(terms(1).astype(HALF_TYPE), dc=1)
        return terms(0) + other.astype(FULL_TYPE)

    def over_z(self, values):
        lines = [
            [(z * self.x_size + x) * CORES + c for z in range(Z_SIZE)]
            for x in range(self.x_size)
            for c in range(CORES)
        ]
        found = lax.psum_scatter(
            values, "row", scatter_dimension=0, axis_index_groups=lines, tiled=True
        )
        return found.astype(FULL_TYPE)

    def over_z_direct(self, values, *earlier):
        blocks = values.reshape((Z_SIZE, -1, values.shape[1]))

        def block(ahead):
            return lax.dynamic_index_in_dim(
                blocks, lax.rem(self.z + ahead, Z_SIZE), 0, keepdims=False
            )

        total = block(0).astype(FULL_TYPE)
        for ahead in range(1, Z_SIZE):
            came = after(self.move(block(ahead), dz=ahead), *earlier)
            total = total + came.astype(FULL_TYPE)
        return total


def after(values, *earlier):
    return lax.optimization_barrier((values, earlier))[0]


class Link:
    def __init__(self, move):
        self.move = move
        self.came = None

    def send(self, values, *earlier, last=True):
        if self.came is not None:
            values = after(values, self.came, *earlier)
        came = self.move(values)
        if last:
            self.came = came
        return (values, came)


class Sum:
    def __init__(self, row, terms):
        self.row = row
        self.terms = terms

    def over_cores(self, dx):
        other = self.row.move(self.terms(dx, 1, ()), dc=1)
        return self.terms(dx, 0, (other,))

    def prepare(self):
        self.total = self.over_cores(self.row.x_size - 1)
        return self.total

    def send(self, *earlier, last=True):
        sent, self.came = self.row.x_link.send(self.total, *earlier, last=last)
        return sent

    def hold(self):
        terms = self.terms(0, 1, ())
        self.other = self.row.move(terms, dc=1)
        return terms

    def finish(self, *earlier):
        came = after(self.came, *earlier)
        for dx in range(self.row.x_size - 2, -1, -1):
            other = self.row.move(self.terms(dx, 1, ()), dc=1) if dx else self.other
            total = self.terms(dx, 0, (other, came))
            if dx:
                came = self.row.move(total, dx=1)
        return total


class Terms:
    def __init__(self, row, across, right_side):
        self.row = row
        self.blocks = across.reshape((Z_SIZE, row.x_size, CORES, -1, across.shape[1]))
        self.right_side = right_side

    def __call__(self, dx, dc, earlier):
        x_at = lax.rem(self.row.x + dx, self.row.x_size)
        core_at = lax.rem(self.row.core + dc, CORES)
        return piece_product(self.blocks, x_at, core_at, self.right_side, earlier)

    def wait(self, *earlier):
        self.right_side = after(self.right_side, *earlier)


def taken_terms(row, rows_of):
    def terms(dx, dc, earlier):
        total = rows_of(lambda array: row.quarter(array, dx, dc)).astype(FULL_TYPE)
        return sum([more.astype(FULL_TYPE) for more in earlier], total).astype(HALF_TYPE)

    return terms


def col_scatter(values, col_count):
    half = values.astype(HALF_TYPE)
    if col_count != 2:
        return lax.psum_scatter(half, "col", scatter_dimension=1, tiled=True).astype(FULL_TYPE)
    width = half.shape[1] // 2
    first = lax.axis_index("col") == 0
    left, right = half[:, :width], half[:, width:]
    other = lax.ppermute(jnp.where(first, right, left), "col", [(0, 1), (1, 0)])
    return jnp.where(first, left, right).astype(FULL_TYPE) + other.astype(FULL_TYPE)


def col_gather(values, col_count):
    if col_count != 2:
        return lax.all_gather(values, "col", axis=1, tiled=True)
    other = lax.ppermute(values, "col", [(0, 1), (1, 0)])
    first = lax.axis_index("col") == 0
    return jnp.concatenate(
        [jnp.where(first, values, other), jnp.where(first, other, values)], axis=1
    )


def col_send(values, col_count):
    half = values.astype(HALF_TYPE)
    if col_count != 2:
        return (half, None)
    return (half, lax.ppermute(half, "col", [(0, 1), (1, 0)]))


def col_sum(pair, *earlier):
    half, other = pair
    if other is None:
        return lax.psum(half.astype(FULL_TYPE), "col")
    other = after(other, *earlier)
    return half.astype(FULL_TYPE) + other.astype(FULL_TYPE)


def heads_apart(weight, heads):
    split = weight.reshape(weight.shape[0], heads, NOPE + ROPE)
    return jnp.concatenate(
        [
            split[:, :, :NOPE].reshape(weight.shape[0], heads * NOPE),
            split[:, :, NOPE:].reshape(weight.shape[0], heads * ROPE),
        ],
        axis=1,
    )


def heads_together(weight, heads):
    rows = weight.shape[0]
    return jnp.concatenate(
        [
            weight[:, : heads * NOPE].reshape(rows, heads, NOPE),
            weight[:, heads * NOPE :].reshape(rows, heads, ROPE),
        ],
        axis=2,
    ).reshape(rows, heads * (NOPE + ROPE))


def fold_count(height, width, rows):
    count = rows // height
    while width % count:
        count -= 1
    return count


def fold_up(weight, devices, rows):
    height = weight.shape[0] // devices
    count = fold_count(height, weight.shape[1], rows)
    width = weight.shape[1] // count
    blocks = [
        weight[:, index * width : (index + 1) * width].reshape(devices, height, width)
        for index in range(count)
    ]
    if count * height < rows:
        blocks.append(jnp.zeros((devices, rows - count * height, width), weight.dtype))
    return jnp.concatenate(blocks, axis=1).reshape(devices * rows, width)


def unfold(folded, devices, height, width):
    rows = folded.shape[0] // devices
    count = fold_count(height, width, rows)
    blocks = folded.reshape(devices, rows, folded.shape[1])
    return jnp.concatenate(
        [
            blocks[:, index * height : (index + 1) * height].reshape(devices * height, -1)
            for index in range(count)
        ],
        axis=1,
    )


GAIN_LANES = 32


def fold_gains(gains, devices, rows):
    flat = gains.reshape(devices, -1)
    short = -flat.shape[1] % GAIN_LANES
    flat = jnp.pad(flat, ((0, 0), (0, short)))
    blocks = flat.reshape(devices, -1, GAIN_LANES)
    blocks = jnp.pad(blocks, ((0, 0), (0, rows - blocks.shape[1]), (0, 0)))
    return blocks.reshape(devices * rows, GAIN_LANES)


def unfold_gains(folded, devices, count):
    flat = folded.reshape(devices, -1)
    return flat[:, :count].reshape(-1)


def body(
    tokens,
    dest_row,
    seq_lens,
    cotangent,
    query_down,
    joint_down,
    query_up,
    joint_up,
    out_weight,
    gate_weight,
    up_weight,
    down_weight,
    norm_gains,
    first_query_down,
    first_joint_down,
    first_query_up,
    first_joint_up,
    first_out_weight,
    first_gate_weight,
    first_up_weight,
    first_down_weight,
    first_norm_gains,
    second_query_down,
    second_joint_down,
    second_query_up,
    second_joint_up,
    second_out_weight,
    second_gate_weight,
    second_up_weight,
    second_down_weight,
    second_norm_gains,
):
    params = (
        query_down,
        joint_down,
        query_up,
        joint_up,
        out_weight,
        gate_weight,
        up_weight,
        down_weight,
        norm_gains,
    )
    firsts = (
        first_query_down,
        first_joint_down,
        first_query_up,
        first_joint_up,
        first_out_weight,
        first_gate_weight,
        first_up_weight,
        first_down_weight,
        first_norm_gains,
    )
    seconds = (
        second_query_down,
        second_joint_down,
        second_query_up,
        second_joint_up,
        second_out_weight,
        second_gate_weight,
        second_up_weight,
        second_down_weight,
        second_norm_gains,
    )
    col_count = lax.axis_size("col")
    col_index = lax.axis_index("col")
    row_count = lax.axis_size("row")
    row = Row(row_count)
    heads = HEADS // col_count
    width_share = D // col_count
    token_count = tokens.shape[0]
    col_start = col_index * width_share
    shard_rows = query_down.shape[0]
    gain_count = norm_gains.shape[0]
    ffn_width = gate_weight.shape[1]

    half = lambda weight: weight.astype(HALF_TYPE)
    parts = [
        half(query_down),
        half(out_weight),
        fold_up(half(joint_up), 1, shard_rows),
        fold_up(heads_apart(half(query_up), heads), 1, shard_rows),
        half(joint_down),
        fold_gains(half(norm_gains), 1, shard_rows),
    ]
    first_width = ffn_width - max(2 * ffn_width // 3 // 256, 1) * 256
    offsets = [3 * first_width]
    for part in parts:
        offsets.append(offsets[-1] + part.shape[1])
    spare = -offsets[-1] % 128
    ffn_weights = [half(gate_weight), half(up_weight), half(down_weight)]
    packed_one = jnp.concatenate(
        [weight[:, :first_width] for weight in ffn_weights]
        + parts
        + [jnp.zeros((shard_rows, spare), HALF_TYPE)],
        axis=1,
    )
    packed_two = jnp.concatenate([weight[:, first_width:] for weight in ffn_weights], axis=1)
    gathered_one = lax.all_gather(packed_one, "row", axis=0, tiled=True)
    gathered_two = lax.all_gather(packed_two, "row", axis=0, tiled=True)
    taken = [gathered_one[:, offsets[i] : offsets[i + 1]] for i in range(6)]
    query_down_all = taken[0]
    out_all = taken[1]
    joint_up_all = unfold(taken[2], row_count, joint_up.shape[0], joint_up.shape[1])
    query_up_all = unfold(taken[3], row_count, query_up.shape[0], query_up.shape[1])
    joint_down_all = taken[4]
    gains_all = unfold_gains(taken[5], row_count, gain_count).astype(FULL_TYPE)
    gain_one = gains_all[:D]
    gain_two = gains_all[D : 2 * D]
    gain_query = gains_all[2 * D : 2 * D + Q_RANK]
    gain_joint = gains_all[2 * D + Q_RANK :]
    query_nope_all = query_up_all[:, : heads * NOPE]
    query_rope_all = query_up_all[:, heads * NOPE :]

    share = token_count // row_count
    target = dest_row // CAP
    local_rows = dest_row - target * CAP
    ids = jnp.arange(token_count, dtype=jnp.int32)
    same_before = (target[:, None] == target[None, :]) & (ids[None, :] < ids[:, None])
    slots = target * share + jnp.sum(same_before.astype(jnp.int32), axis=1)
    sends = slots[None, :] == ids[:, None]
    send_matrix = sends.astype(HALF_TYPE)
    sorted_rows = jnp.sum(jnp.where(sends, local_rows[None, :], 0), axis=1)
    sorted_tokens = product(send_matrix, tokens).astype(HALF_TYPE)
    arrived_rows = lax.all_to_all(
        sorted_rows, "row", split_axis=0, concat_axis=0, tiled=True
    )
    arrived = lax.all_to_all(sorted_tokens, "row", split_axis=0, concat_axis=0, tiled=True)

    lengths = seq_lens[0]
    padded = (lengths + BLK - 1) // BLK * BLK
    endings = CAP - jnp.sum(padded) + jnp.cumsum(padded)
    starts = endings - lengths
    inside = (arrived_rows[:, None] >= starts[None, :]) & (
        arrived_rows[:, None] < endings[None, :]
    )
    first_rows = jnp.sum(jnp.where(inside, starts[None, :], 0), axis=1)
    position = (arrived_rows - first_rows).astype(FULL_TYPE)
    frequency = 10000.0 ** (-(jnp.arange(ROPE // 2, dtype=FULL_TYPE) * 2.0 / ROPE))
    angles = position[:, None] * frequency[None, :]
    cosine = jnp.tile(jnp.cos(angles), (1, 2))
    sine = jnp.tile(jnp.sin(angles), (1, 2))
    group = head_group(heads)
    places = (
        arrived_rows[:, None],
        arrived_rows[None, :],
        first_rows[None, :],
        jnp.tile(cosine, (1, group)),
        jnp.tile(sine, (1, group)),
    )
    row_matrix = (
        jnp.arange(CAP, dtype=jnp.int32)[:, None] == arrived_rows[None, :]
    ).astype(HALF_TYPE)
    upstream_part = contract_rows(row_matrix, cotangent).astype(HALF_TYPE)

    features = col_gather(arrived, col_count)
    upstream = col_gather(upstream_part, col_count).astype(FULL_TYPE)
    ffn_grad = (RESIDUAL_SCALE * upstream).astype(HALF_TYPE)

    inputs = features.astype(FULL_TYPE)
    scale_one = rms_scale(inputs)
    normed_one = (inputs * scale_one * gain_one).astype(HALF_TYPE)
    query_latent = product(normed_one, query_down_all)
    joint_latent = product(normed_one, joint_down_all)
    scale_query = rms_scale(query_latent)
    query_normed = (query_latent * scale_query * gain_query).astype(HALF_TYPE)
    compressed_raw = joint_latent[:, :KV_RANK]
    scale_joint = rms_scale(compressed_raw)
    compressed = (compressed_raw * scale_joint * gain_joint).astype(HALF_TYPE)
    rope_raw = joint_latent[:, KV_RANK:]
    key_rope = (rope_raw * cosine + rotate_half(rope_raw) * sine).astype(HALF_TYPE)
    query_nope = product(query_normed, query_nope_all).astype(HALF_TYPE)
    query_rope = product(query_normed, query_rope_all)
    joint_full = product(compressed, joint_up_all).astype(HALF_TYPE)
    attended, rotated, log_totals = attention_forward(
        places, key_rope, query_nope, query_rope, joint_full, heads
    )
    branch = col_sum(col_send(times_transposed(attended, out_all), col_count))
    residual = inputs + RESIDUAL_SCALE * branch

    scale_two = rms_scale(residual)
    normed_two = (residual * scale_two * gain_two).astype(HALF_TYPE)
    ffn_grad_across = ffn_grad.T
    normed_two_across = normed_two.T
    normed_one_across = normed_one.T
    activated, grad_gate, grad_up = feed_part(normed_two, ffn_grad, gathered_one, first_width)
    down_sum = Sum(row, Terms(row, ffn_grad_across, activated))
    both_sum = Sum(
        row, Terms(row, normed_two_across, jnp.concatenate([grad_gate, grad_up], axis=1))
    )
    down_sum.prepare()
    down_sum.send()
    both_sum.prepare()
    held = (down_sum.hold(), both_sum.hold())
    forward_one = across_part([activated], [2], gathered_one, [], FULL_TYPE)
    backward_one = across_part([grad_gate, grad_up], [0, 1], gathered_one, [], FULL_TYPE)
    both_sent = both_sum.send(held)
    down_one = down_sum.finish(both_sent, forward_one, backward_one)
    gathered_two = after(gathered_two, forward_one, backward_one, down_one)

    activated, grad_gate, grad_up = feed_part(
        normed_two, ffn_grad, gathered_two, ffn_width - first_width
    )
    down_terms = Terms(row, ffn_grad_across, activated)
    gate_terms = Terms(row, normed_two_across, grad_gate)
    up_terms = Terms(row, normed_two_across, grad_up)
    down_sum = Sum(row, down_terms)
    gate_sum = Sum(row, gate_terms)
    up_sum = Sum(row, up_terms)
    down_sum.prepare()
    gate_total = gate_sum.prepare()
    down_sent = down_sum.send(gate_total)

    one_grads = row.over_z(jnp.concatenate([both_sum.finish(down_sent), down_one], axis=1))
    grad_gate, grad_up = after((grad_gate, grad_up), down_sent)
    backward_two = across_part(
        [grad_gate, grad_up], [0, 1], gathered_two, [backward_one], HALF_TYPE
    )
    up_terms.wait(backward_two)
    up_total = up_sum.prepare()
    grad_normed_two = col_send(backward_two, col_count)
    activated = after(activated, up_total)
    forward_two = across_part([activated], [2], gathered_two, [forward_one], HALF_TYPE)
    down_terms.wait(forward_two)
    gate_terms.wait(forward_two)
    held = (down_sum.hold(), gate_sum.hold())
    gate_sent = gate_sum.send(up_total, held)

    down_two = row.over_z(down_sum.finish(gate_sent))
    grad_normed_two = col_sum(grad_normed_two, gate_sent)
    through_two, gain_two_grad = rms_backward(grad_normed_two, residual, scale_two, gain_two)
    grad_residual = upstream + through_two
    branch_grad = (RESIDUAL_SCALE * grad_residual).astype(HALF_TYPE)
    out_sum = Sum(row, Terms(row, branch_grad.T, attended))
    out_total = out_sum.prepare()
    branch_grad = after(branch_grad, out_total)
    grad_attended = product(branch_grad, out_all).astype(HALF_TYPE)

    grad_nope, grad_rope, grad_joint_full, grad_key = attention_backward(
        places, key_rope, query_nope, rotated, joint_full, grad_attended, log_totals, heads
    )
    up_sent = up_sum.send(grad_joint_full)
    grad_nope, grad_rope, grad_joint_full = after(
        (grad_nope, grad_rope, grad_joint_full), up_sent
    )
    gate_two = row.over_z(gate_sum.finish(up_sent))
    query_up_grad = jnp.concatenate(
        [contract_rows(query_normed, grad_nope), contract_rows(query_normed, grad_rope)], axis=1
    )
    joint_up_grad = contract_rows(compressed, grad_joint_full)
    folded_grads = jnp.concatenate(
        [
            fold_up(query_up_grad.astype(HALF_TYPE), row_count, shard_rows),
            fold_up(joint_up_grad.astype(HALF_TYPE), row_count, shard_rows),
        ],
        axis=1,
    )
    up_terms.wait(grad_joint_full)
    held = up_sum.hold()
    heads_sum = Sum(row, taken_terms(row, lambda take: take(folded_grads)))
    heads_total = heads_sum.prepare()
    latents = col_send(
        jnp.concatenate(
            [
                times_transposed(grad_nope, query_nope_all)
                + times_transposed(grad_rope, query_rope_all),
                times_transposed(grad_joint_full, joint_up_all),
                grad_key,
            ],
            axis=1,
        ),
        col_count,
    )
    latents = col_sum(latents)
    grad_query_normed = latents[:, :Q_RANK]
    grad_compressed = latents[:, Q_RANK : Q_RANK + KV_RANK]
    grad_rope_sum = latents[:, Q_RANK + KV_RANK :]
    grad_query_latent, gain_query_grad = rms_backward(
        grad_query_normed, query_latent, scale_query, gain_query
    )
    grad_compressed_raw, gain_joint_grad = rms_backward(
        grad_compressed, compressed_raw, scale_joint, gain_joint
    )
    grad_key_raw = grad_rope_sum * cosine + rotate_back(grad_rope_sum * sine)
    grad_latents = jnp.concatenate(
        [grad_query_latent, grad_compressed_raw, grad_key_raw], axis=1
    ).astype(HALF_TYPE)
    grad_normed_one = times_transposed(
        grad_latents[:, :Q_RANK], query_down_all
    ) + times_transposed(grad_latents[:, Q_RANK:], joint_down_all)
    through_one, gain_one_grad = rms_backward(grad_normed_one, inputs, scale_one, gain_one)
    grad_inputs = lax.dynamic_slice_in_dim(
        grad_residual + through_one, col_start, width_share, 1
    ).astype(HALF_TYPE)
    gains_grad = fold_gains(
        jnp.concatenate([gain_one_grad, gain_two_grad, gain_query_grad, gain_joint_grad]),
        row_count,
        shard_rows,
    )
    downs_sum = Sum(
        row,
        taken_terms(
            row,
            lambda take: jnp.concatenate(
                [product(take(normed_one_across), grad_latents), take(gains_grad)], axis=1
            ),
        ),
    )
    downs_total = downs_sum.prepare()
    out_sent = out_sum.send(heads_total, held, downs_total, last=False)
    heads_sent = heads_sum.send(last=False)
    downs_sent = downs_sum.send(last=False)

    up_two = row.over_z(up_sum.finish(out_sent))
    returned = lax.all_to_all(
        after(grad_inputs, out_sent), "row", split_axis=0, concat_axis=0, tiled=True
    )
    grad_tokens = contract_rows(send_matrix, returned).astype(HALF_TYPE)
    feed_forward = col_scatter(after(forward_two, out_sent), col_count)
    residual_part = lax.dynamic_slice_in_dim(residual, col_start, width_share, 1)
    output_rows = residual_part + RESIDUAL_SCALE * feed_forward
    output_pad = product(row_matrix, output_rows.astype(HALF_TYPE)).astype(HALF_TYPE)
    out_sum.hold()
    heads_sum.hold()
    downs_sum.hold()
    out_total = out_sum.finish(heads_sent, downs_sent)
    heads_total = heads_sum.finish(downs_sent)
    downs_total = downs_sum.finish()
    out_grad = row.over_z_direct(out_total, downs_total)
    heads_grad = row.over_z_direct(heads_total, downs_total)
    downs_grad = row.over_z_direct(downs_total)
    gate_grad, up_grad, down_grad = [
        jnp.concatenate(
            [one_grads[:, index * first_width : (index + 1) * first_width], two], axis=1
        )
        for index, two in enumerate((gate_two, up_two, down_two))
    ]
    query_fold = taken[3].shape[1]
    reduced = (
        downs_grad[:, :Q_RANK],
        downs_grad[:, Q_RANK : Q_RANK + KV_RANK + ROPE],
        heads_together(
            unfold(heads_grad[:, :query_fold], 1, query_up.shape[0], query_up.shape[1]), heads
        ),
        unfold(heads_grad[:, query_fold:], 1, joint_up.shape[0], joint_up.shape[1]),
        out_grad,
        gate_grad,
        up_grad,
        down_grad,
        unfold_gains(downs_grad[:, Q_RANK + KV_RANK + ROPE :], 1, gain_count),
    )
    step_rates = learning_rates()
    seconds_next = []
    weights_next = []
    for slot_index in range(9):
        second_new, weight_new = adam_update(
            params[slot_index],
            reduced[slot_index],
            firsts[slot_index],
            seconds[slot_index],
            step_rates[slot_index],
        )
        seconds_next.append(second_new)
        weights_next.append(weight_new)
    return (output_pad, grad_tokens) + reduced + tuple(seconds_next) + tuple(weights_next)


def solution(mesh):
    in_specs = (
        P("row", "col"),
        P("row"),
        P("row", None),
        P("row", "col"),
        P("row", None),
        P("row", None),
        P("row", "col"),
        P("row", "col"),
        P("row", "col"),
        P("row", "col"),
        P("row", "col"),
        P("row", "col"),
        P("row"),
        P("row", None),
        P("row", None),
        P("row", "col"),
        P("row", "col"),
        P("row", "col"),
        P("row", "col"),
        P("row", "col"),
        P("row", "col"),
        P("row"),
        P("row", None),
        P("row", None),
        P("row", "col"),
        P("row", "col"),
        P("row", "col"),
        P("row", "col"),
        P("row", "col"),
        P("row", "col"),
        P("row"),
    )
    out_specs = (
        P("row", "col"),
        P("row", "col"),
        P("row", None),
        P("row", None),
        P("row", "col"),
        P("row", "col"),
        P("row", "col"),
        P("row", "col"),
        P("row", "col"),
        P("row", "col"),
        P("row"),
        P("row", None),
        P("row", None),
        P("row", "col"),
        P("row", "col"),
        P("row", "col"),
        P("row", "col"),
        P("row", "col"),
        P("row", "col"),
        P("row"),
        P("row", None),
        P("row", None),
        P("row", "col"),
        P("row", "col"),
        P("row", "col"),
        P("row", "col"),
        P("row", "col"),
        P("row", "col"),
        P("row"),
    )
    return jax.shard_map(body, mesh=mesh, in_specs=in_specs, out_specs=out_specs, check_vma=False)
```

```python
import functools

import jax
import jax.numpy as jnp
from jax import lax
from jax.experimental import pallas as pl
from jax.experimental.pallas import tpu as pltpu
from jax.sharding import PartitionSpec as P

D = 2560
FF = 6400
HEADS = 40
NOPE = 64
ROPE = 32
VDIM = 64
Q_RANK = 768
KV_RANK = 256
SEQS = 4
BLK = 128
STEP = 10
CAP = 896

Z_SIZE = 4
CORES = 2

EPSILON = 1e-05
RESIDUAL_SCALE = 1.4 / 62**0.5
BETA_ONE = 0.9
BETA_TWO = 0.95
ADAM_EPSILON = 1e-08
DECAY_RATE = 0.1
MASKED = -1e30
SCORE_SCALE = (NOPE + ROPE) ** (-0.5)
FULL_TYPE = jnp.float32
HALF_TYPE = jnp.bfloat16


def rms_scale(values):
    return lax.rsqrt(jnp.mean(values * values, axis=-1, keepdims=True) + EPSILON)


def rms_backward(grad_normed, values, norm_scale, gain_values):
    weighted = grad_normed * gain_values
    mean_term = jnp.mean(weighted * values, axis=-1, keepdims=True)
    grad_values = norm_scale * weighted - values * norm_scale**3 * mean_term
    grad_gain = jnp.sum(grad_normed * values * norm_scale, axis=0)
    return (grad_values, grad_gain)


def product(left_side, right_side):
    return jnp.dot(left_side, right_side, preferred_element_type=FULL_TYPE)


def contract_rows(left_side, right_side):
    return lax.dot_general(
        left_side, right_side, (((0,), (0,)), ((), ())), preferred_element_type=FULL_TYPE
    )


def times_transposed(left_side, right_side):
    return lax.dot_general(
        left_side, right_side, (((1,), (1,)), ((), ())), preferred_element_type=FULL_TYPE
    )


def rotate_half(values):
    half_width = values.shape[-1] // 2
    return jnp.concatenate([-values[..., half_width:], values[..., :half_width]], axis=-1)


def rotate_back(values):
    half_width = values.shape[-1] // 2
    return jnp.concatenate([values[..., half_width:], -values[..., :half_width]], axis=-1)


def learning_rates():
    return (
        3.0 * D ** (-0.5),
        3.0 * D ** (-0.5),
        3.0 * (Q_RANK // 2) ** (-0.5),
        3.0 * KV_RANK ** (-0.5),
        3.0 * max(HEADS * VDIM // 512, 1) ** (-0.5),
        3.0 * D ** (-0.5),
        3.0 * D ** (-0.5),
        3.0 * max(FF // 80, 1) ** (-0.5),
        0.6,
    )


def adam_update(weight_old, grad_value, first_old, second_old, step_rate):
    first_new = BETA_ONE * first_old + (1.0 - BETA_ONE) * grad_value
    second_new = BETA_TWO * second_old + (1.0 - BETA_TWO) * grad_value * grad_value
    first_hat = first_new / (1.0 - BETA_ONE**STEP)
    second_hat = second_new / (1.0 - BETA_TWO**STEP)
    weight_new = weight_old - step_rate * (
        first_hat / (jnp.sqrt(second_hat) + ADAM_EPSILON) + DECAY_RATE * weight_old
    )
    return (second_new, weight_new)


def turn_matrix(width):
    rows = lax.broadcasted_iota(jnp.int32, (width, width), 0)
    columns = lax.broadcasted_iota(jnp.int32, (width, width), 1)
    half = ROPE // 2
    in_first = (columns % ROPE) < half
    minus = in_first & (rows == columns + half)
    plus = jnp.logical_not(in_first) & (rows == columns - half)
    return jnp.where(plus, 1.0, jnp.where(minus, -1.0, 0.0)).astype(HALF_TYPE)


def split_dot(values, matrix, dims):
    high = values.astype(HALF_TYPE)
    low = (values - high.astype(FULL_TYPE)).astype(HALF_TYPE)
    dot = functools.partial(
        lax.dot_general, dimension_numbers=(dims, ((), ())), preferred_element_type=FULL_TYPE
    )
    return dot(high, matrix) + dot(low, matrix)


NT = ((1,), (1,))
NN = ((1,), (0,))


def kernel_dot(left_side, right_side, dims):
    return lax.dot_general(
        left_side, right_side, (dims, ((), ())), preferred_element_type=FULL_TYPE
    )


def fill_bias(bias_ref, row_here, row_across, first_across):
    key_rows = row_here[...]
    allowed = (key_rows >= first_across[...]) & (key_rows <= row_across[...])
    bias_ref[...] = jnp.where(allowed, 0.0, MASKED)


def attend_kernel(
    group,
    row_here,
    row_across,
    first_across,
    cosine,
    sine,
    key_rope,
    query_nope,
    query_rope,
    joint,
    attended,
    rotated,
    totals,
    bias,
):
    @pl.when(pl.program_id(0) == 0)
    def _():
        fill_bias(bias, row_here, row_across, first_across)

    turn = turn_matrix(group * ROPE)
    rope_in = query_rope[...]
    rotated[...] = (
        rope_in * cosine[...] + split_dot(rope_in, turn, NN) * sine[...]
    ).astype(HALF_TYPE)
    rope_keys = key_rope[...]
    for head in range(group):
        keys = joint[:, head * 128 : head * 128 + NOPE]
        values = joint[:, head * 128 + NOPE : (head + 1) * 128]
        scores = (
            kernel_dot(keys, query_nope[:, head * NOPE : (head + 1) * NOPE], NT)
            + kernel_dot(rope_keys, rotated[:, head * ROPE : (head + 1) * ROPE], NT)
        ) * SCORE_SCALE + bias[...]
        top = jnp.max(scores, axis=0, keepdims=True)
        powers = jnp.exp(scores - top)
        total = jnp.sum(powers, axis=0, keepdims=True)
        weights = (powers * (1.0 / total)).astype(HALF_TYPE)
        found = kernel_dot(values.T, weights, NN)
        attended[:, head * VDIM : (head + 1) * VDIM] = found.T.astype(HALF_TYPE)
        totals[0, head : head + 1, :] = top + jnp.log(total)


def attend_back_kernel(
    group,
    row_here,
    row_across,
    first_across,
    cosine,
    sine,
    key_rope,
    query_nope,
    rotated,
    joint,
    grad_out,
    totals,
    grad_nope,
    grad_rope,
    grad_joint,
    grad_key,
    bias,
):
    @pl.when(pl.program_id(0) == 0)
    def _():
        fill_bias(bias, row_here, row_across, first_across)
        grad_key[...] = jnp.zeros_like(grad_key)

    turn = turn_matrix(group * ROPE)
    rope_keys = key_rope[...]
    rope_keys_across = rope_keys.T
    rope_grads = []
    key_grad = jnp.zeros(grad_key.shape, FULL_TYPE)
    for head in range(group):
        keys = joint[:, head * 128 : head * 128 + NOPE]
        values = joint[:, head * 128 + NOPE : (head + 1) * 128]
        queries = query_nope[:, head * NOPE : (head + 1) * NOPE]
        turned = rotated[:, head * ROPE : (head + 1) * ROPE]
        out_grad = grad_out[:, head * VDIM : (head + 1) * VDIM]
        scores = (
            kernel_dot(keys, queries, NT) + kernel_dot(rope_keys, turned, NT)
        ) * SCORE_SCALE + bias[...]
        probs = jnp.exp(scores - totals[0, head : head + 1, :])
        value_grad = kernel_dot(probs.astype(HALF_TYPE), out_grad, NN)
        prob_grad = kernel_dot(values, out_grad, NT)
        delta = jnp.sum(probs * prob_grad, axis=0, keepdims=True)
        score_grad = (probs * (prob_grad - delta)).astype(HALF_TYPE)
        nope_key_grad = kernel_dot(score_grad, queries, NN) * SCORE_SCALE
        key_grad = key_grad + kernel_dot(score_grad, turned, NN)
        query_grad = kernel_dot(keys.T, score_grad, NN) * SCORE_SCALE
        rope_grads.append(kernel_dot(rope_keys_across, score_grad, NN))
        grad_nope[:, head * NOPE : (head + 1) * NOPE] = query_grad.T.astype(HALF_TYPE)
        grad_joint[:, head * 128 : head * 128 + NOPE] = nope_key_grad.astype(HALF_TYPE)
        grad_joint[:, head * 128 + NOPE : (head + 1) * 128] = value_grad.astype(HALF_TYPE)
    rope_grad = jnp.concatenate(rope_grads, axis=0).T * SCORE_SCALE
    grad_rope[...] = (
        rope_grad * cosine[...] + split_dot(rope_grad * sine[...], turn, NT)
    ).astype(HALF_TYPE)
    grad_key[...] += key_grad * SCORE_SCALE


def head_group(heads):
    return 4 if heads % 4 == 0 else heads


def attention_specs(tokens, group):
    whole = lambda *shape: pl.BlockSpec(shape, lambda step: (0,) * len(shape))
    wide = lambda width: pl.BlockSpec((tokens, width), lambda step: (0, step))
    shared = [
        whole(tokens, 1),
        whole(1, tokens),
        whole(1, tokens),
        whole(tokens, group * ROPE),
        whole(tokens, group * ROPE),
        whole(tokens, ROPE),
    ]
    totals = pl.BlockSpec((1, group, tokens), lambda step: (step, 0, 0))
    return (whole, wide, shared, totals)


def attention_forward(places, key_rope, query_nope, query_rope, joint, heads):
    tokens = joint.shape[0]
    group = head_group(heads)
    _, wide, shared, totals = attention_specs(tokens, group)
    return pl.pallas_call(
        functools.partial(attend_kernel, group),
        grid=(heads // group,),
        in_specs=shared + [wide(group * NOPE), wide(group * ROPE), wide(group * 128)],
        out_specs=[wide(group * VDIM), wide(group * ROPE), totals],
        out_shape=[
            jax.ShapeDtypeStruct((tokens, heads * VDIM), HALF_TYPE),
            jax.ShapeDtypeStruct((tokens, heads * ROPE), HALF_TYPE),
            jax.ShapeDtypeStruct((heads // group, group, tokens), FULL_TYPE),
        ],
        scratch_shapes=[pltpu.VMEM((tokens, tokens), FULL_TYPE)],
        compiler_params=pltpu.CompilerParams(vmem_limit_bytes=40 << 20),
        cost_estimate=cost(heads * tokens * tokens * 1000, query_rope, joint, query_nope),
    )(*places, key_rope, query_nope, query_rope, joint)


def attention_backward(places, key_rope, query_nope, rotated, joint, grad_out, log_totals, heads):
    tokens = joint.shape[0]
    group = head_group(heads)
    whole, wide, shared, totals = attention_specs(tokens, group)
    return pl.pallas_call(
        functools.partial(attend_back_kernel, group),
        grid=(heads // group,),
        in_specs=shared
        + [wide(group * NOPE), wide(group * ROPE), wide(group * 128), wide(group * VDIM), totals],
        out_specs=[
            wide(group * NOPE),
            wide(group * ROPE),
            wide(group * 128),
            whole(tokens, ROPE),
        ],
        out_shape=[
            jax.ShapeDtypeStruct((tokens, heads * NOPE), HALF_TYPE),
            jax.ShapeDtypeStruct((tokens, heads * ROPE), HALF_TYPE),
            jax.ShapeDtypeStruct((tokens, heads * 128), HALF_TYPE),
            jax.ShapeDtypeStruct((tokens, ROPE), FULL_TYPE),
        ],
        scratch_shapes=[pltpu.VMEM((tokens, tokens), FULL_TYPE)],
        compiler_params=pltpu.CompilerParams(vmem_limit_bytes=40 << 20),
        cost_estimate=cost(heads * tokens * tokens * 2000, joint, joint, grad_out, grad_out),
    )(*places, key_rope, query_nope, rotated, joint, grad_out, log_totals)


LANES = 128
KERNEL_MEMORY = 58 << 20


def tile_of(width, most):
    return max(
        (tile for tile in range(LANES, most + 1, LANES) if width % tile == 0), default=None
    )


def cost(flops, *arrays):
    moved = sum(array.size * array.dtype.itemsize for array in arrays)
    return pl.CostEstimate(flops=flops, bytes_accessed=moved, transcendentals=0)


def feed_terms(gate_rows, up_rows, grad_act):
    sigmoid_gate = 1.0 / (1.0 + jnp.exp(-gate_rows))
    silu = gate_rows * sigmoid_gate
    activated = silu * up_rows
    grad_gate = grad_act * up_rows * sigmoid_gate * (1.0 + gate_rows * (1.0 - sigmoid_gate))
    return [value.astype(HALF_TYPE) for value in (activated, grad_gate, grad_act * silu)]


def feed_kernel(share, normed, ffn_grad, gate, up, down, activated, grad_gate, grad_up):
    gate_rows = kernel_dot(normed[...], gate[...], NN)
    up_rows = kernel_dot(normed[...], up[...], NN)
    grad_act = kernel_dot(ffn_grad[...], down[...], NN)
    activated[...], grad_gate[...], grad_up[...] = feed_terms(gate_rows, up_rows, grad_act)


def feed_part(normed, ffn_grad, gathered, width, shares=1, share=0):
    tokens, depth = normed.shape
    tile = tile_of(width, 512)
    if tile is None:
        gate, up, down = [
            lax.dynamic_slice_in_dim(gathered, (index * shares + share) * width, width, 1)
            for index in range(3)
        ]
        return feed_terms(product(normed, gate), product(normed, up), product(ffn_grad, down))
    count = width // tile
    whole = pl.BlockSpec((tokens, depth), lambda step, share: (0, 0))
    part = lambda index: pl.BlockSpec(
        (depth, tile), lambda step, share: (0, (index * shares + share[0]) * count + step)
    )
    return pl.pallas_call(
        feed_kernel,
        grid_spec=pltpu.PrefetchScalarGridSpec(
            num_scalar_prefetch=1,
            grid=(count,),
            in_specs=[whole, whole, part(0), part(1), part(2)],
            out_specs=[pl.BlockSpec((tokens, tile), lambda step, share: (0, step))] * 3,
        ),
        out_shape=[jax.ShapeDtypeStruct((tokens, width), HALF_TYPE)] * 3,
        compiler_params=pltpu.CompilerParams(vmem_limit_bytes=KERNEL_MEMORY),
        cost_estimate=cost(6 * tokens * depth * width, normed, ffn_grad, gathered),
    )(jnp.full((1,), share, jnp.int32), normed, ffn_grad, gathered, gathered, gathered)


def across_kernel(count, share, *refs):
    total = kernel_dot(refs[0][...], refs[count][...], NT)
    for index in range(1, count):
        total = total + kernel_dot(refs[index][...], refs[count + index][...], NT)
    refs[-1][...] = total.astype(refs[-1].dtype)


def across_part(sides, places, gathered, kind, shares=1, share=0):
    tokens, width = sides[0].shape
    depth = gathered.shape[0]
    if width % LANES:
        total = sum(
            times_transposed(
                side,
                lax.dynamic_slice_in_dim(gathered, (place * shares + share) * width, width, 1),
            )
            for side, place in zip(sides, places, strict=True)
        )
        return total.astype(kind)
    tile = tile_of(depth, 512)
    rows = lambda place: pl.BlockSpec(
        (tile, width), lambda step, share: (step, place * shares + share[0])
    )
    return pl.pallas_call(
        functools.partial(across_kernel, len(sides)),
        grid_spec=pltpu.PrefetchScalarGridSpec(
            num_scalar_prefetch=1,
            grid=(depth // tile,),
            in_specs=[pl.BlockSpec((tokens, width), lambda step, share: (0, 0))] * len(sides)
            + [rows(place) for place in places],
            out_specs=pl.BlockSpec((tokens, tile), lambda step, share: (0, step)),
        ),
        out_shape=jax.ShapeDtypeStruct((tokens, depth), kind),
        compiler_params=pltpu.CompilerParams(vmem_limit_bytes=KERNEL_MEMORY),
        cost_estimate=cost(2 * len(sides) * tokens * depth * width, *sides),
    )(jnp.full((1,), share, jnp.int32), *sides, *[gathered] * len(sides))


def piece_kernel(places, left_side, right_side, *refs):
    rows = left_side[...].reshape(-1, left_side.shape[-1])
    total = kernel_dot(rows, right_side[...], NN)
    for more in refs[:-1]:
        total = total + more[...].astype(FULL_TYPE)
    refs[-1][...] = total.astype(HALF_TYPE)


def piece_product(blocks, x_at, core_at, right_side, earlier, every_x=False):
    z_size, x_count, _, rows, tokens = blocks.shape
    x_count = x_count if every_x else 1
    width = right_side.shape[1]
    tile = tile_of(width, 1280)
    if tile is None or rows % 16:
        left_side = lax.dynamic_slice(
            blocks, (0, x_at, core_at, 0, 0), (z_size, x_count, 1, rows, tokens)
        )
        total = product(left_side.reshape(-1, tokens), right_side)
        return sum([more.astype(FULL_TYPE) for more in earlier], total).astype(HALF_TYPE)
    height = z_size * x_count * rows
    block = pl.BlockSpec((height, tile), lambda step, places: (0, step))
    return pl.pallas_call(
        piece_kernel,
        grid_spec=pltpu.PrefetchScalarGridSpec(
            num_scalar_prefetch=1,
            grid=(width // tile,),
            in_specs=[
                pl.BlockSpec(
                    (z_size, x_count, 1, rows, tokens),
                    lambda step, places: (0, places[0], places[1], 0, 0),
                ),
                pl.BlockSpec((tokens, tile), lambda step, places: (0, step)),
            ]
            + [block] * len(earlier),
            out_specs=block,
        ),
        out_shape=jax.ShapeDtypeStruct((height, width), HALF_TYPE),
        compiler_params=pltpu.CompilerParams(vmem_limit_bytes=KERNEL_MEMORY),
        cost_estimate=cost(
            2 * height * tokens * width, right_side, right_side, right_side, *earlier
        ),
    )(jnp.stack([x_at, core_at]).astype(jnp.int32), blocks, right_side, *earlier)


class Row:
    def __init__(self, size):
        self.size = size
        self.x_size = size // (Z_SIZE * CORES)
        index = lax.axis_index("row")
        self.z = index // (self.x_size * CORES)
        self.x = (index // CORES) % self.x_size
        self.core = index % CORES
        self.x_link = Link(functools.partial(self.move, dx=1))

    def move(self, values, dz=0, dx=0, dc=0):
        def at(z, x, c):
            return ((z % Z_SIZE) * self.x_size + x % self.x_size) * CORES + c % CORES

        pairs = [
            (at(z, x, c), at(z + dz, x + dx, c + dc))
            for z in range(Z_SIZE)
            for x in range(self.x_size)
            for c in range(CORES)
        ]
        return lax.ppermute(values, "row", pairs)

    def quarter(self, array, dx, dc):
        blocks = array.reshape(
            (Z_SIZE, self.x_size, CORES, array.shape[0] // self.size, array.shape[1])
        )
        x_at = lax.rem(self.x + dx, self.x_size)
        core_at = lax.rem(self.core + dc, CORES)
        part = lax.dynamic_slice(
            blocks,
            (0, x_at, core_at, 0, 0),
            (Z_SIZE, 1, 1) + blocks.shape[3:],
        )
        return part.reshape((-1, array.shape[1]))

    def halves(self, array, dc):
        blocks = array.reshape(
            (Z_SIZE * self.x_size, CORES, array.shape[0] // self.size, array.shape[1])
        )
        part = lax.dynamic_slice_in_dim(blocks, lax.rem(self.core + dc, CORES), 1, 1)
        return part.reshape((-1, array.shape[1]))

    def over_cores(self, terms):
        other = self.move(terms(1).astype(HALF_TYPE), dc=1)
        return terms(0) + other.astype(FULL_TYPE)

    def over_z(self, values):
        lines = [
            [(z * self.x_size + x) * CORES + c for z in range(Z_SIZE)]
            for x in range(self.x_size)
            for c in range(CORES)
        ]
        found = lax.psum_scatter(
            values, "row", scatter_dimension=0, axis_index_groups=lines, tiled=True
        )
        return found.astype(FULL_TYPE)

    def by_core(self, halves, axis):
        first = self.core == 0
        keep = jnp.where(first, halves[0], halves[1])
        came = self.move(jnp.where(first, halves[1], halves[0]), dc=1)
        return jnp.concatenate(
            [jnp.where(first, keep, came), jnp.where(first, came, keep)], axis=axis
        )

    def begun(self, values):
        return self.move(values[:16, :LANES], dc=1)

    def with_other(self, values):
        return jnp.concatenate([values, self.move(values, dc=1)], axis=0)

    def own_half(self, values, *earlier):
        count = values.shape[0] // CORES
        came = after(self.move(values[count:], dc=1), *earlier)
        return values[:count].astype(FULL_TYPE) + came.astype(FULL_TYPE)

    def x_last(self, values):
        blocks = values.reshape((self.x_size, -1, values.shape[1]))

        def block(ahead):
            return lax.dynamic_index_in_dim(
                blocks, lax.rem(self.x + ahead, self.x_size), 0, keepdims=False
            )

        total = block(self.x_size - 1)
        for step in range(1, self.x_size):
            came = self.move(total.astype(HALF_TYPE), dx=1)
            total = came.astype(FULL_TYPE) + block(self.x_size - 1 - step)
        return total


def after(values, *earlier):
    if not earlier:
        return values
    values = lax.optimization_barrier((values, earlier))[0]
    return lax.optimization_barrier((values, earlier))[0]


class Link:
    def __init__(self, move):
        self.move = move
        self.came = None

    def send(self, values, *earlier, last=True):
        if self.came is not None:
            values = after(values, self.came, *earlier)
        came = self.move(values)
        if last:
            self.came = came
        return (values, came)


class Sum:
    def __init__(self, row, terms):
        self.row = row
        self.terms = terms

    def share(self, *earlier):
        terms = after(self.terms(self.row.x_size - 1, 1, ()), *earlier)
        self.shared = self.row.move(terms, dc=1)
        return terms

    def prepare(self):
        self.total = self.terms(self.row.x_size - 1, 0, (self.shared,))
        return self.total

    def send(self, *earlier, last=True):
        sent, self.came = self.row.x_link.send(self.total, *earlier, last=last)
        return self.row.begun(sent)

    def hold(self):
        terms = self.terms(0, 1, ())
        self.other = self.row.move(terms, dc=1)
        return terms

    def finish(self, *earlier):
        came = after(self.came, *earlier)
        for dx in range(self.row.x_size - 2, -1, -1):
            other = self.row.move(self.terms(dx, 1, ()), dc=1) if dx else self.other
            total = self.terms(dx, 0, (other, came))
            if dx:
                came = self.row.move(total, dx=1)
        return total


class WideSum:
    def __init__(self, row, terms):
        self.row = row
        self.terms = terms

    def prepare(self):
        self.total = self.terms(self.row.x_size - 1, 0, ())
        return self.total

    def send(self, *earlier):
        sent, self.came = self.row.x_link.send(self.total, *earlier)
        return self.row.begun(sent)

    def finish(self, *earlier):
        came = after(self.came, *earlier)
        for dx in range(self.row.x_size - 2, -1, -1):
            total = self.terms(dx, 0, (came,))
            if dx:
                came = self.row.move(total, dx=1)
        return total


class Terms:
    def __init__(self, row, across, right_side, cores=CORES):
        self.row = row
        self.cores = cores
        self.blocks = across.reshape((Z_SIZE, row.x_size, cores, -1, across.shape[1]))
        self.right_side = right_side

    def __call__(self, dx, dc, earlier):
        x_at = lax.rem(self.row.x + dx, self.row.x_size)
        core_at = lax.rem(self.row.core + dc, CORES) if self.cores > 1 else jnp.int32(0)
        return piece_product(self.blocks, x_at, core_at, self.right_side, earlier)

    def wait(self, *earlier):
        self.right_side = after(self.right_side, *earlier)

    def every_x(self, dc, earlier):
        core_at = lax.rem(self.row.core + dc, CORES)
        return piece_product(
            self.blocks, jnp.int32(0), core_at, self.right_side, earlier, every_x=True
        )


def terms_and_taken(terms, row, array, width):
    total = terms.right_side.shape[1]

    def both(dx, dc, earlier):
        more = row.quarter(array, dx, dc).astype(HALF_TYPE)
        more = jnp.pad(more, ((0, 0), (width, total - width - array.shape[1])))
        return terms(dx, dc, (*earlier, more))

    return both


def taken_terms(row, rows_of):
    def terms(dx, dc, earlier):
        total = rows_of(lambda array: row.quarter(array, dx, dc)).astype(FULL_TYPE)
        return sum([more.astype(FULL_TYPE) for more in earlier], total).astype(HALF_TYPE)

    return terms


def col_scatter(values, col_count):
    half = values.astype(HALF_TYPE)
    if col_count != 2:
        return lax.psum_scatter(half, "col", scatter_dimension=1, tiled=True).astype(FULL_TYPE)
    width = half.shape[1] // 2
    first = lax.axis_index("col") == 0
    left, right = half[:, :width], half[:, width:]
    other = lax.ppermute(jnp.where(first, right, left), "col", [(0, 1), (1, 0)])
    return jnp.where(first, left, right).astype(FULL_TYPE) + other.astype(FULL_TYPE)


def col_gather(values, col_count):
    if col_count != 2:
        return lax.all_gather(values, "col", axis=1, tiled=True)
    other = lax.ppermute(values, "col", [(0, 1), (1, 0)])
    first = lax.axis_index("col") == 0
    return jnp.concatenate(
        [jnp.where(first, values, other), jnp.where(first, other, values)], axis=1
    )


def col_send(values, col_count):
    half = values.astype(HALF_TYPE)
    if col_count != 2:
        return (half, None)
    return (half, lax.ppermute(half, "col", [(0, 1), (1, 0)]))


def col_sum(pair, *earlier):
    half, other = pair
    if other is None:
        return lax.psum(half.astype(FULL_TYPE), "col")
    other = after(other, *earlier)
    return half.astype(FULL_TYPE) + other.astype(FULL_TYPE)


def heads_apart(weight, heads):
    split = weight.reshape(weight.shape[0], heads, NOPE + ROPE)
    return jnp.concatenate(
        [
            split[:, :, :NOPE].reshape(weight.shape[0], heads * NOPE),
            split[:, :, NOPE:].reshape(weight.shape[0], heads * ROPE),
        ],
        axis=1,
    )


def heads_together(weight, heads):
    rows = weight.shape[0]
    return jnp.concatenate(
        [
            weight[:, : heads * NOPE].reshape(rows, heads, NOPE),
            weight[:, heads * NOPE :].reshape(rows, heads, ROPE),
        ],
        axis=2,
    ).reshape(rows, heads * (NOPE + ROPE))


def fold_count(height, width, rows):
    count = rows // height
    while width % count:
        count -= 1
    return count


def fold_up(weight, devices, rows):
    height = weight.shape[0] // devices
    count = fold_count(height, weight.shape[1], rows)
    width = weight.shape[1] // count
    blocks = [
        weight[:, index * width : (index + 1) * width].reshape(devices, height, width)
        for index in range(count)
    ]
    if count * height < rows:
        blocks.append(jnp.zeros((devices, rows - count * height, width), weight.dtype))
    return jnp.concatenate(blocks, axis=1).reshape(devices * rows, width)


def unfold(folded, devices, height, width):
    rows = folded.shape[0] // devices
    count = fold_count(height, width, rows)
    blocks = folded.reshape(devices, rows, folded.shape[1])
    return jnp.concatenate(
        [
            blocks[:, index * height : (index + 1) * height].reshape(devices * height, -1)
            for index in range(count)
        ],
        axis=1,
    )


GAIN_LANES = 32


def fold_gains(gains, devices, rows):
    flat = gains.reshape(devices, -1)
    short = -flat.shape[1] % GAIN_LANES
    flat = jnp.pad(flat, ((0, 0), (0, short)))
    blocks = flat.reshape(devices, -1, GAIN_LANES)
    blocks = jnp.pad(blocks, ((0, 0), (0, rows - blocks.shape[1]), (0, 0)))
    return blocks.reshape(devices * rows, GAIN_LANES)


def unfold_gains(folded, devices, count):
    flat = folded.reshape(devices, -1)
    return flat[:, :count].reshape(-1)


def body(
    tokens,
    dest_row,
    seq_lens,
    cotangent,
    query_down,
    joint_down,
    query_up,
    joint_up,
    out_weight,
    gate_weight,
    up_weight,
    down_weight,
    norm_gains,
    first_query_down,
    first_joint_down,
    first_query_up,
    first_joint_up,
    first_out_weight,
    first_gate_weight,
    first_up_weight,
    first_down_weight,
    first_norm_gains,
    second_query_down,
    second_joint_down,
    second_query_up,
    second_joint_up,
    second_out_weight,
    second_gate_weight,
    second_up_weight,
    second_down_weight,
    second_norm_gains,
):
    params = (
        query_down,
        joint_down,
        query_up,
        joint_up,
        out_weight,
        gate_weight,
        up_weight,
        down_weight,
        norm_gains,
    )
    firsts = (
        first_query_down,
        first_joint_down,
        first_query_up,
        first_joint_up,
        first_out_weight,
        first_gate_weight,
        first_up_weight,
        first_down_weight,
        first_norm_gains,
    )
    seconds = (
        second_query_down,
        second_joint_down,
        second_query_up,
        second_joint_up,
        second_out_weight,
        second_gate_weight,
        second_up_weight,
        second_down_weight,
        second_norm_gains,
    )
    col_count = lax.axis_size("col")
    col_index = lax.axis_index("col")
    row_count = lax.axis_size("row")
    row = Row(row_count)
    heads = HEADS // col_count
    width_share = D // col_count
    token_count = tokens.shape[0]
    col_start = col_index * width_share
    shard_rows = query_down.shape[0]
    gain_count = norm_gains.shape[0]
    ffn_width = gate_weight.shape[1]

    half = lambda weight: weight.astype(HALF_TYPE)
    parts = [
        half(query_down),
        half(out_weight),
        fold_up(half(joint_up), 1, shard_rows),
        fold_up(heads_apart(half(query_up), heads), 1, shard_rows),
        half(joint_down),
        fold_gains(half(norm_gains), 1, shard_rows),
    ]
    first_width = ffn_width - max(2 * ffn_width // 3 // 256, 1) * 256
    offsets = [3 * first_width]
    for part in parts:
        offsets.append(offsets[-1] + part.shape[1])
    spare = -offsets[-1] % 128
    ffn_weights = [half(gate_weight), half(up_weight), half(down_weight)]
    packed_one = jnp.concatenate(
        [weight[:, :first_width] for weight in ffn_weights]
        + parts
        + [jnp.zeros((shard_rows, spare), HALF_TYPE)],
        axis=1,
    )
    second_width = (ffn_width - first_width) // CORES
    packed_two = jnp.concatenate([weight[:, first_width:] for weight in ffn_weights], axis=1)
    gathered_one = lax.all_gather(packed_one, "row", axis=0, tiled=True)
    gathered_two = lax.all_gather(packed_two, "row", axis=0, tiled=True)
    taken = [gathered_one[:, offsets[i] : offsets[i + 1]] for i in range(6)]
    query_down_all = taken[0]
    out_all = taken[1]
    joint_up_all = unfold(taken[2], row_count, joint_up.shape[0], joint_up.shape[1])
    query_up_all = unfold(taken[3], row_count, query_up.shape[0], query_up.shape[1])
    joint_down_all = taken[4]
    gains_all = unfold_gains(taken[5], row_count, gain_count).astype(FULL_TYPE)
    gain_one = gains_all[:D]
    gain_two = gains_all[D : 2 * D]
    gain_query = gains_all[2 * D : 2 * D + Q_RANK]
    gain_joint = gains_all[2 * D + Q_RANK :]
    query_nope_all = query_up_all[:, : heads * NOPE]
    query_rope_all = query_up_all[:, heads * NOPE :]

    share = token_count // row_count
    target = dest_row // CAP
    local_rows = dest_row - target * CAP
    ids = jnp.arange(token_count, dtype=jnp.int32)
    same_before = (target[:, None] == target[None, :]) & (ids[None, :] < ids[:, None])
    slots = target * share + jnp.sum(same_before.astype(jnp.int32), axis=1)
    sends = slots[None, :] == ids[:, None]
    send_matrix = sends.astype(HALF_TYPE)
    sorted_rows = jnp.sum(jnp.where(sends, local_rows[None, :], 0), axis=1)
    sorted_tokens = product(send_matrix, tokens).astype(HALF_TYPE)
    arrived_rows = lax.all_to_all(
        sorted_rows, "row", split_axis=0, concat_axis=0, tiled=True
    )
    arrived = lax.all_to_all(sorted_tokens, "row", split_axis=0, concat_axis=0, tiled=True)

    lengths = seq_lens[0]
    padded = (lengths + BLK - 1) // BLK * BLK
    endings = CAP - jnp.sum(padded) + jnp.cumsum(padded)
    starts = endings - lengths
    inside = (arrived_rows[:, None] >= starts[None, :]) & (
        arrived_rows[:, None] < endings[None, :]
    )
    first_rows = jnp.sum(jnp.where(inside, starts[None, :], 0), axis=1)
    position = (arrived_rows - first_rows).astype(FULL_TYPE)
    frequency = 10000.0 ** (-(jnp.arange(ROPE // 2, dtype=FULL_TYPE) * 2.0 / ROPE))
    angles = position[:, None] * frequency[None, :]
    cosine = jnp.tile(jnp.cos(angles), (1, 2))
    sine = jnp.tile(jnp.sin(angles), (1, 2))
    group = head_group(heads)
    places = (
        arrived_rows[:, None],
        arrived_rows[None, :],
        first_rows[None, :],
        jnp.tile(cosine, (1, group)),
        jnp.tile(sine, (1, group)),
    )
    row_matrix = (
        jnp.arange(CAP, dtype=jnp.int32)[:, None] == arrived_rows[None, :]
    ).astype(HALF_TYPE)
    upstream_part = contract_rows(row_matrix, cotangent).astype(HALF_TYPE)

    features = col_gather(arrived, col_count)
    upstream = col_gather(upstream_part, col_count).astype(FULL_TYPE)
    ffn_grad = (RESIDUAL_SCALE * upstream).astype(HALF_TYPE)

    inputs = features.astype(FULL_TYPE)
    scale_one = rms_scale(inputs)
    normed_one = (inputs * scale_one * gain_one).astype(HALF_TYPE)
    query_latent = product(normed_one, query_down_all)
    joint_latent = product(normed_one, joint_down_all)
    scale_query = rms_scale(query_latent)
    query_normed = (query_latent * scale_query * gain_query).astype(HALF_TYPE)
    compressed_raw = joint_latent[:, :KV_RANK]
    scale_joint = rms_scale(compressed_raw)
    compressed = (compressed_raw * scale_joint * gain_joint).astype(HALF_TYPE)
    rope_raw = joint_latent[:, KV_RANK:]
    key_rope = (rope_raw * cosine + rotate_half(rope_raw) * sine).astype(HALF_TYPE)
    query_nope = product(query_normed, query_nope_all).astype(HALF_TYPE)
    query_rope = product(query_normed, query_rope_all)
    joint_full = product(compressed, joint_up_all).astype(HALF_TYPE)
    attended, rotated, log_totals = attention_forward(
        places, key_rope, query_nope, query_rope, joint_full, heads
    )
    branch = col_sum(col_send(times_transposed(attended, out_all), col_count))
    residual = inputs + RESIDUAL_SCALE * branch

    scale_two = rms_scale(residual)
    normed_two = (residual * scale_two * gain_two).astype(HALF_TYPE)
    ffn_grad_across = ffn_grad.T
    ffn_grad_pair = row.with_other(ffn_grad)
    normed_two_across = normed_two.T
    normed_one_across = normed_one.T
    activated, grad_gate, grad_up = feed_part(normed_two, ffn_grad, gathered_one, first_width)
    down_sum = Sum(row, Terms(row, ffn_grad_across, activated))
    both_terms = Terms(
        row, normed_two_across, jnp.concatenate([grad_gate, grad_up], axis=1)
    )
    down_sum.share()
    both_shared = both_terms.every_x(1, ())
    down_sum.prepare()
    down_sum.send()
    both_total = both_terms.every_x(0, (row.move(both_shared, dc=1),))
    both_found = row.over_z(both_total)
    held = down_sum.hold()
    forward_one = across_part([activated], [2], gathered_one, FULL_TYPE)
    backward_one = across_part([grad_gate, grad_up], [0, 1], gathered_one, FULL_TYPE)
    normed_pair = row.with_other(normed_two)
    normed_pair_across = normed_pair.T
    ffn_grad_pair_across = ffn_grad_pair.T
    down_one = down_sum.finish(
        both_total, forward_one, backward_one, normed_pair_across, ffn_grad_pair_across
    )
    down_one_grad = row.over_z(down_one)
    gathered_two = after(gathered_two, down_one)

    activated, grad_gate, grad_up = feed_part(
        normed_pair, ffn_grad_pair, gathered_two, second_width, CORES, row.core
    )
    down_sum = WideSum(row, Terms(row, ffn_grad_pair_across, activated, 1))
    gate_sum = WideSum(row, Terms(row, normed_pair_across, grad_gate, 1))
    up_sum = WideSum(row, Terms(row, normed_pair_across, grad_up, 1))
    down_sum.prepare()
    down_sent = down_sum.send()

    grad_gate, grad_up = after((grad_gate, grad_up), down_sent)
    backward_two = across_part(
        [grad_gate, grad_up], [0, 1], gathered_two, HALF_TYPE, CORES, row.core
    )
    pair = col_send(row.own_half(backward_two) + backward_one, col_count)
    y_sent = row.begun(pair[0])
    gate_sum.terms.wait(y_sent)
    gate_total = gate_sum.prepare()
    up_sum.terms.wait(gate_total)
    up_total = up_sum.prepare()
    activated = after(activated, up_total)
    forward_two = across_part([activated], [2], gathered_two, HALF_TYPE, CORES, row.core)
    grad_normed_two = col_sum(pair, forward_two)
    gate_sent = gate_sum.send(grad_normed_two)

    down_total = down_sum.finish(gate_sent)
    down_two = row.over_z(after(down_total, both_found))
    one_grads = row.x_last(after(both_found, down_total))
    grad_normed_two = after(grad_normed_two, down_total)
    through_two, gain_two_grad = rms_backward(grad_normed_two, residual, scale_two, gain_two)
    grad_residual = upstream + through_two
    branch_grad = (RESIDUAL_SCALE * grad_residual).astype(HALF_TYPE)
    out_sum = Sum(row, Terms(row, branch_grad.T, attended))
    shared = out_sum.share()
    out_total = out_sum.prepare()
    out_sum.terms.wait(out_total)
    held = out_sum.hold()
    branch_grad = after(branch_grad, shared)
    grad_attended = product(branch_grad, out_all).astype(HALF_TYPE)
    feed_forward = col_scatter(
        row.own_half(after(forward_two, down_total)) + forward_one, col_count
    )
    residual_part = lax.dynamic_slice_in_dim(residual, col_start, width_share, 1)
    output_rows = residual_part + RESIDUAL_SCALE * feed_forward
    output_pad = product(row_matrix, output_rows.astype(HALF_TYPE)).astype(HALF_TYPE)

    grad_nope, grad_rope, grad_joint_full, grad_key = attention_backward(
        places, key_rope, query_nope, rotated, joint_full, grad_attended, log_totals, heads
    )
    up_sent = up_sum.send(grad_joint_full, held, output_pad, one_grads)

    gate_total = gate_sum.finish(up_sent)
    gate_two = row.over_z(gate_total)
    grad_nope, grad_rope, grad_joint_full = after(
        (grad_nope, grad_rope, grad_joint_full), gate_total
    )
    query_up_grad = jnp.concatenate(
        [contract_rows(query_normed, grad_nope), contract_rows(query_normed, grad_rope)], axis=1
    )
    joint_up_grad = contract_rows(compressed, grad_joint_full)
    folded_grads = jnp.concatenate(
        [
            fold_up(query_up_grad.astype(HALF_TYPE), row_count, shard_rows),
            fold_up(joint_up_grad.astype(HALF_TYPE), row_count, shard_rows),
        ],
        axis=1,
    )
    latents = col_send(
        jnp.concatenate(
            [
                times_transposed(grad_nope, query_nope_all)
                + times_transposed(grad_rope, query_rope_all),
                times_transposed(grad_joint_full, joint_up_all),
                grad_key,
            ],
            axis=1,
        ),
        col_count,
    )
    heads_sum = Sum(row, taken_terms(row, lambda take: take(folded_grads)))
    heads_sum.share()
    heads_sum.hold()
    latents = col_sum(latents)
    grad_query_normed = latents[:, :Q_RANK]
    grad_compressed = latents[:, Q_RANK : Q_RANK + KV_RANK]
    grad_rope_sum = latents[:, Q_RANK + KV_RANK :]
    grad_query_latent, gain_query_grad = rms_backward(
        grad_query_normed, query_latent, scale_query, gain_query
    )
    grad_compressed_raw, gain_joint_grad = rms_backward(
        grad_compressed, compressed_raw, scale_joint, gain_joint
    )
    grad_key_raw = grad_rope_sum * cosine + rotate_back(grad_rope_sum * sine)
    grad_latents = jnp.concatenate(
        [grad_query_latent, grad_compressed_raw, grad_key_raw], axis=1
    ).astype(HALF_TYPE)
    grad_normed_one = times_transposed(
        grad_latents[:, :Q_RANK], query_down_all
    ) + times_transposed(grad_latents[:, Q_RANK:], joint_down_all)
    through_one, gain_one_grad = rms_backward(grad_normed_one, inputs, scale_one, gain_one)
    grad_inputs = lax.dynamic_slice_in_dim(
        grad_residual + through_one, col_start, width_share, 1
    ).astype(HALF_TYPE)
    gains_grad = fold_gains(
        jnp.concatenate([gain_one_grad, gain_two_grad, gain_query_grad, gain_joint_grad]),
        row_count,
        shard_rows,
    )
    latent_width = grad_latents.shape[1] // col_count
    latent_part = lax.dynamic_slice_in_dim(
        grad_latents, col_index * latent_width, latent_width, 1
    )
    filled = -(latent_width + GAIN_LANES) % LANES + GAIN_LANES
    downs_terms = Terms(
        row, normed_one_across, jnp.pad(latent_part, ((0, 0), (0, filled)))
    )
    downs_sum = Sum(row, terms_and_taken(downs_terms, row, gains_grad, latent_width))
    heads_total = heads_sum.prepare()
    out_sent = out_sum.send(heads_total, last=False)
    heads_sent = heads_sum.send(last=False)

    up_total = up_sum.finish(out_sent)
    up_two = row.over_z(up_total)
    downs_terms.wait(up_total, heads_sent)
    downs_sum.share()
    downs_sum.hold()
    downs_sum.prepare()
    downs_sent = downs_sum.send(last=False)
    returned = lax.all_to_all(
        after(grad_inputs, downs_sent), "row", split_axis=0, concat_axis=0, tiled=True
    )
    out_total = out_sum.finish(up_total)
    grad_tokens = contract_rows(send_matrix, returned).astype(HALF_TYPE)
    heads_total = heads_sum.finish(out_total, downs_sent)
    downs_total = downs_sum.finish(heads_total)
    last_grad = row.over_z(jnp.concatenate([out_total, heads_total, downs_total], axis=1))
    gate_grad, up_grad, down_grad = [
        jnp.concatenate(
            [
                one,
                row.by_core(
                    [two[:shard_rows].astype(HALF_TYPE), two[shard_rows:].astype(HALF_TYPE)],
                    axis=1,
                ).astype(FULL_TYPE),
            ],
            axis=1,
        )
        for one, two in (
            (one_grads[:, :first_width], gate_two),
            (one_grads[:, first_width:], up_two),
            (down_one_grad, down_two),
        )
    ]
    step_rates = learning_rates()
    updated = {
        slot: adam_update(params[slot], grad, firsts[slot], seconds[slot], step_rates[slot])
        for slot, grad in ((5, gate_grad), (6, up_grad), (7, down_grad))
    }
    out_grad = last_grad[:, : out_total.shape[1]]
    heads_grad = last_grad[:, out_total.shape[1] : -downs_total.shape[1]]
    downs_part = last_grad[:, -downs_total.shape[1] :]
    downs_grad = col_gather(downs_part[:, :latent_width].astype(HALF_TYPE), col_count)
    downs_grad = downs_grad.astype(FULL_TYPE)
    gains_found = downs_part[:, latent_width : latent_width + GAIN_LANES]
    query_fold = taken[3].shape[1]
    reduced = (
        downs_grad[:, :Q_RANK],
        downs_grad[:, Q_RANK : Q_RANK + KV_RANK + ROPE],
        heads_together(
            unfold(heads_grad[:, :query_fold], 1, query_up.shape[0], query_up.shape[1]), heads
        ),
        unfold(heads_grad[:, query_fold:], 1, joint_up.shape[0], joint_up.shape[1]),
        out_grad,
        gate_grad,
        up_grad,
        down_grad,
        unfold_gains(gains_found, 1, gain_count),
    )
    seconds_next = []
    weights_next = []
    for slot_index in range(9):
        second_new, weight_new = updated.get(slot_index) or adam_update(
            params[slot_index],
            reduced[slot_index],
            firsts[slot_index],
            seconds[slot_index],
            step_rates[slot_index],
        )
        seconds_next.append(second_new)
        weights_next.append(weight_new)
    return (output_pad, grad_tokens) + reduced + tuple(seconds_next) + tuple(weights_next)


def solution(mesh):
    in_specs = (
        P("row", "col"),
        P("row"),
        P("row", None),
        P("row", "col"),
        P("row", None),
        P("row", None),
        P("row", "col"),
        P("row", "col"),
        P("row", "col"),
        P("row", "col"),
        P("row", "col"),
        P("row", "col"),
        P("row"),
        P("row", None),
        P("row", None),
        P("row", "col"),
        P("row", "col"),
        P("row", "col"),
        P("row", "col"),
        P("row", "col"),
        P("row", "col"),
        P("row"),
        P("row", None),
        P("row", None),
        P("row", "col"),
        P("row", "col"),
        P("row", "col"),
        P("row", "col"),
        P("row", "col"),
        P("row", "col"),
        P("row"),
    )
    out_specs = (
        P("row", "col"),
        P("row", "col"),
        P("row", None),
        P("row", None),
        P("row", "col"),
        P("row", "col"),
        P("row", "col"),
        P("row", "col"),
        P("row", "col"),
        P("row", "col"),
        P("row"),
        P("row", None),
        P("row", None),
        P("row", "col"),
        P("row", "col"),
        P("row", "col"),
        P("row", "col"),
        P("row", "col"),
        P("row", "col"),
        P("row"),
        P("row", None),
        P("row", None),
        P("row", "col"),
        P("row", "col"),
        P("row", "col"),
        P("row", "col"),
        P("row", "col"),
        P("row", "col"),
        P("row"),
    )
    return jax.shard_map(body, mesh=mesh, in_specs=in_specs, out_specs=out_specs, check_vma=False)
```
